128 devices in a mesh: dp: 8 (over y, core), ctx: 16 (over x, z).
Axes of the slice: x: 4, y: 4, z: 4, core: 2. Of those that a mesh axis runs over, the one named last changes fastest.
Arguments:
- queries: bfloat16 [8, 4096, 4096], P('dp', 'ctx'), may hold values from -6 to 6
- keys_in: bfloat16 [8, 4096, 4096], P('dp', 'ctx'), may hold values from -6 to 6
- values_in: bfloat16 [8, 4096, 4096], P('dp', 'ctx'), may hold values from -6 to 6
- filters: float32 [4096, 4096], P('ctx'), may hold values from -0.09375 to 0.09375
- skip_gain: float32 [4096], replicated, may hold values from -4 to 4
- out_weight: bfloat16 [4096, 4096], P(None, ('dp', 'ctx')), may hold values from -0.09375 to 0.09375
Outputs:
- projected: bfloat16 [8, 4096, 4096], P('dp', 'ctx')
The draws below stay inside these ranges and needn't reach their ends.
All inputs are finite; a program needn't handle non-finite values.
Results may differ from the reference program's by a relative error of at most 0.0064.
Values may be sent and summed in bfloat16 or wider, within the bound.
No kernel may reach another device: no remote copies, remote signals or barrier semaphores. Data moves between devices by JAX's collectives and lax.ppermute only.
A program may use at most 256 MiB of HBM per device.

```python
import jax
import jax.numpy as jnp
from jax import lax

C = 4096
DO = 4096
L = 4096
B = 8


def levels(own_key, shape, pieces, low, largest):
    level = 1.0
    for position, blocks in pieces:
        steps = jax.random.uniform(jax.random.fold_in(jax.random.fold_in(own_key, 6), position), (blocks,), jnp.float32, low / len(pieces), largest / len(pieces))
        level = level * jnp.repeat(jnp.exp(steps), shape[position] // blocks).reshape((-1,) + (1,) * (len(shape) - 1 - position))
    return level


def bell_draw(own_key, dims, deviation, most, pieces=(), held_as=jnp.bfloat16):
    values = jax.random.normal(own_key, dims, jnp.float32) * deviation
    if len(pieces) > 0:
        values = levels(own_key, dims, pieces, -0.22, 0.18) * values
    return jnp.clip(values, min=-most, max=most).astype(held_as)


def setup_inputs(seed: int = 0) -> dict:
    seeds = jax.random.split(jax.random.key(seed), 7)
    return {
        "queries": bell_draw(seeds[0], (B, L, C), 1.0, 6.0, ((0, 8), (1, 16))),
        "keys_in": bell_draw(seeds[1], (B, L, C), 1.0, 6.0, ((0, 8), (1, 16))),
        "values_in": bell_draw(seeds[2], (B, L, C), 1.0, 6.0, ((0, 8), (1, 16))),
        "filters": bell_draw(seeds[3], (C, L), L ** -0.5, 0.09375, ((0, 16),), jnp.float32),
        "skip_gain": bell_draw(seeds[4], (C,), 1.0, 4.0, (), jnp.float32),
        "out_weight": bell_draw(seeds[5], (C, DO), C ** -0.5, 0.09375, ((1, 128),)),
    }


def reference(queries, keys_in, values_in, filters, skip_gain, out_weight):
    filter_spec = jnp.fft.rfft(filters.astype(jnp.float32), n=2 * L, axis=1).T

    def one_sequence(items):
        query_seq, key_seq, value_seq = items
        product = (key_seq.astype(jnp.float32) * value_seq.astype(jnp.float32)).astype(jnp.bfloat16)
        product = lax.optimization_barrier(product)
        signal = product.astype(jnp.float32)
        spectrum = jnp.fft.rfft(signal, n=2 * L, axis=0)
        causal = jnp.fft.irfft(spectrum * filter_spec, n=2 * L, axis=0)[:L]
        mixed = (causal + skip_gain[None, :] * signal).astype(jnp.bfloat16)
        mixed = lax.optimization_barrier(mixed)
        gated = (query_seq.astype(jnp.float32) * mixed.astype(jnp.float32)).astype(jnp.bfloat16)
        return jnp.dot(gated, out_weight, preferred_element_type=jnp.float32).astype(jnp.bfloat16)

    return lax.map(one_sequence, (queries, keys_in, values_in))
```

```python
import math

import jax
import jax.numpy as jnp
import ml_dtypes
import numpy as np
from jax import lax
from jax.experimental import pallas as pl
from jax.experimental.pallas import tpu as pltpu
from jax.sharding import PartitionSpec as P

F32 = jnp.float32
BF16 = jnp.bfloat16
MIB = 1024 * 1024

OUTER = 32
INNER = 128


def split_table(table):
    high = table.astype(ml_dtypes.bfloat16)
    low = (table - high.astype(np.float64)).astype(ml_dtypes.bfloat16)
    return high, low


def tables():
    length = OUTER * INNER
    k1 = np.arange(OUTER)[:, None, None]
    k2 = np.arange(INNER)[None, :, None]
    b = np.arange(INNER)[None, None, :]
    theta = 2.0 * math.pi * b * (k1 + 0.25 + OUTER * k2) / length
    cos, sin = np.cos(theta), np.sin(theta)
    top = np.concatenate([cos, sin], axis=2)
    bottom = np.concatenate([-sin, cos], axis=2)
    forward = np.concatenate([top, bottom], axis=1)
    backward = np.swapaxes(forward, 1, 2) / length
    return split_table(forward) + split_table(backward)


def cadd(u, v):
    return (u[0] + v[0], u[1] + v[1])


def csub(u, v):
    return (u[0] - v[0], u[1] - v[1])


def turn(u, angle):
    quarter = round(angle / (math.pi / 2), 9)
    if quarter == int(quarter):
        quarter = int(quarter) % 4
        if quarter == 0:
            return u
        if quarter == 1:
            return (-u[1], u[0])
        if quarter == 2:
            return (-u[0], -u[1])
        return (u[1], -u[0])
    c, s = math.cos(angle), math.sin(angle)
    return (u[0] * c - u[1] * s, u[0] * s + u[1] * c)


def four(u, sign):
    p, q = cadd(u[0], u[2]), csub(u[0], u[2])
    r, t = cadd(u[1], u[3]), csub(u[1], u[3])
    if sign < 0:
        t = (t[1], -t[0])
    else:
        t = (-t[1], t[0])
    return [cadd(p, r), cadd(q, t), csub(p, r), csub(q, t)]


def eight(u, sign):
    even = four(u[0::2], sign)
    odd = four(u[1::2], sign)
    half = math.sqrt(0.5)
    o1, o3 = odd[1], odd[3]
    if sign < 0:
        odd[1] = ((o1[0] + o1[1]) * half, (o1[1] - o1[0]) * half)
        odd[2] = (odd[2][1], -odd[2][0])
        odd[3] = ((o3[1] - o3[0]) * half, (o3[0] + o3[1]) * -half)
    else:
        odd[1] = ((o1[0] - o1[1]) * half, (o1[0] + o1[1]) * half)
        odd[2] = (-odd[2][1], odd[2][0])
        odd[3] = ((o3[0] + o3[1]) * -half, (o3[0] - o3[1]) * half)
    return [cadd(even[i], odd[i]) for i in range(4)] + [csub(even[i], odd[i]) for i in range(4)]


def outer_forward(x):
    c1, s1 = math.cos(math.pi / 8), math.sin(math.pi / 8)
    half = math.sqrt(0.5)
    rows = []
    for r in range(8):
        x0, x1, x2, x3 = x[r], x[r + 8], x[r + 16], x[r + 24]
        x2 = x2 * half
        y0, y1 = (x0 + x2, -x2), (x0 - x2, x2)
        u1, v1 = x1 * c1, x1 * s1
        u3, v3 = x3 * s1, x3 * c1
        p = (u1 + u3, -(v1 + v3))
        d = (u1 - u3, v3 - v1)
        d = (d[1], -d[0])
        rows.append([cadd(y0, p), cadd(y1, d), csub(y0, p), csub(y1, d)])
    out = [None] * OUTER
    for q in range(4):
        column = [turn(rows[r][q], -2.0 * math.pi * r * (q + 0.25) / OUTER) for r in range(8)]
        for k, value in enumerate(eight(column, -1)):
            out[q + 4 * k] = value
    return out


def outer_backward(t):
    columns = []
    for q in range(4):
        g = eight([t[q + 4 * k] for k in range(8)], 1)
        columns.append([turn(g[r], 2.0 * math.pi * r * (q + 0.25) / OUTER) for r in range(8)])
    out = [None] * OUTER
    for r in range(8):
        v = [columns[q][r] for q in range(4)]
        p, s = cadd(v[0], v[2]), csub(v[0], v[2])
        w, d = cadd(v[1], v[3]), csub(v[1], v[3])
        out[r] = p[0] + w[0]
        for j, (re, im) in (
            (1, (s[0] - d[1], s[1] + d[0])),
            (2, csub(p, w)),
            (3, (s[0] + d[1], s[1] - d[0])),
        ):
            c, n = math.cos(math.pi * j / 8), math.sin(math.pi * j / 8)
            out[r + 8 * j] = re * c - im * n
    return out


def split(value):
    high = value.astype(BF16)
    return high, (value - high.astype(F32)).astype(BF16)


def close_dot(high, low, value):
    value_high, value_low = split(value)
    return (
        jnp.dot(high, value_high, preferred_element_type=F32)
        + jnp.dot(high, value_low, preferred_element_type=F32)
        + jnp.dot(low, value_high, preferred_element_type=F32)
    )


def product_kernel(keys_ref, values_ref, out_ref):
    out_ref[0] = (keys_ref[...].astype(F32) * values_ref[...].astype(F32)).astype(BF16)


def product_blocks(keys, values, parts):
    rows, width = keys.shape
    cols = width // parts
    return pl.pallas_call(
        product_kernel,
        grid=(parts,),
        in_specs=[pl.BlockSpec((rows, cols), lambda j: (0, j))] * 2,
        out_specs=pl.BlockSpec((1, rows, cols), lambda j: (j, 0, 0)),
        out_shape=jax.ShapeDtypeStruct((parts, rows, cols), BF16),
        cost_estimate=pl.CostEstimate(flops=rows * width, bytes_accessed=6 * rows * width, transcendentals=0),
        name="product",
    )(keys, values)


def spectrum_kernel(filters_ref, high_ref, low_ref, out_ref, taps, high, low, sems):
    chunks = 8
    step = OUTER // chunks

    def fetch(i):
        part = pl.ds(i * step, step)
        return (
            pltpu.make_async_copy(high_ref.at[part], high.at[part], sems.at[0, i]),
            pltpu.make_async_copy(low_ref.at[part], low.at[part], sems.at[1, i]),
        )

    for i in range(chunks):
        for copy in fetch(i):
            copy.start()
    for a in range(OUTER):
        taps[pl.ds(a * INNER, INNER), :] = filters_ref[:, pl.ds(a * INNER, INNER)].T

    def outer(i, carry):
        base = pl.multiple_of(i * 8, 8)
        x = [taps[pl.ds(a * INNER + base, 8), :] for a in range(OUTER)]
        for k, (re, im) in enumerate(outer_forward(x)):
            out_ref[k, pl.ds(base, 8), :] = re
            out_ref[k, pl.ds(INNER + base, 8), :] = im
        return carry

    lax.fori_loop(0, INNER // 8, outer, 0)
    for i in range(chunks):
        for copy in fetch(i):
            copy.wait()

        def inner(k, carry):
            out_ref[k] = close_dot(high[k], low[k], out_ref[k])
            return carry

        lax.fori_loop(i * step, (i + 1) * step, inner, 0)


def filter_spectrum(filters, high, low):
    channels, length = filters.shape
    lanes = 128
    size = 2 * INNER
    return pl.pallas_call(
        spectrum_kernel,
        grid=(channels // lanes,),
        in_specs=[
            pl.BlockSpec((lanes, length), lambda j: (j, 0)),
            pl.BlockSpec(memory_space=pl.ANY),
            pl.BlockSpec(memory_space=pl.ANY),
        ],
        out_specs=pl.BlockSpec((OUTER, size, lanes), lambda j: (0, 0, j)),
        out_shape=jax.ShapeDtypeStruct((OUTER, size, channels), F32),
        scratch_shapes=[
            pltpu.VMEM((length, lanes), F32),
            pltpu.VMEM((OUTER, size, size), BF16),
            pltpu.VMEM((OUTER, size, size), BF16),
            pltpu.SemaphoreType.DMA((2, 8)),
        ],
        compiler_params=pltpu.CompilerParams(vmem_limit_bytes=40 * MIB),
        cost_estimate=pl.CostEstimate(
            flops=6 * OUTER * size * size * channels, bytes_accessed=16 * OUTER * size * size, transcendentals=0
        ),
        name="spectrum",
    )(filters, high, low)


def conv_kernel(
    signal_ref, spec_ref, skip_ref, fh_ref, fl_ref, bh_ref, bl_ref, out_ref, work, spec, fh, fl, bh, bl, sems
):
    chunks = 8
    step = OUTER // chunks
    lanes = 128
    channels = out_ref.shape[1]
    pairs = ((fh_ref, fh), (fl_ref, fl), (spec_ref, spec), (bh_ref, bh), (bl_ref, bl))

    def fetch(i):
        part = pl.ds(i * step, step)
        return [
            pltpu.make_async_copy(source.at[part], target.at[part], sems.at[n, i])
            for n, (source, target) in enumerate(pairs)
        ]

    for i in range(chunks):
        for copy in fetch(i):
            copy.start()

    for c in range(0, channels, lanes):
        col = pl.ds(c, lanes)

        def outer(i, carry):
            base = pl.multiple_of(i * 16, 16)
            rows = [signal_ref[pl.ds(a * INNER + base, 16), col].astype(F32) for a in range(OUTER)]
            for h in range(0, 16, 8):
                for k, (re, im) in enumerate(outer_forward([row[h : h + 8] for row in rows])):
                    work[k, pl.ds(base + h, 8), col] = re
                    work[k, pl.ds(INNER + base + h, 8), col] = im
            return carry

        lax.fori_loop(0, INNER // 16, outer, 0)

    for i in range(chunks):
        for copy in fetch(i):
            copy.wait()

        def inner(k, carry):
            value = close_dot(fh[k], fl[k], work[k])
            re, im = value[:INNER], value[INNER:]
            sre, sim = spec[k, :INNER], spec[k, INNER:]
            mixed = jnp.concatenate([re * sre - im * sim, re * sim + im * sre], axis=0)
            work[k] = close_dot(bh[k], bl[k], mixed)
            return carry

        lax.fori_loop(i * step, (i + 1) * step, inner, 0)

    for c in range(0, channels, lanes):
        col = pl.ds(c, lanes)
        gain = skip_ref[:, col]

        def back(i, carry):
            base = pl.multiple_of(i * 16, 16)
            halves = []
            for h in range(0, 16, 8):
                t = [
                    (work[k, pl.ds(base + h, 8), col], work[k, pl.ds(INNER + base + h, 8), col])
                    for k in range(OUTER)
                ]
                halves.append(outer_backward(t))
            for a in range(OUTER):
                rows = pl.ds(a * INNER + base, 16)
                causal = jnp.concatenate([halves[0][a], halves[1][a]], axis=0)
                out_ref[rows, col] = (causal + gain * signal_ref[rows, col].astype(F32)).astype(BF16)
            return carry

        lax.fori_loop(0, INNER // 16, back, 0)


def convolve(signal, spec, skip, table):
    length, channels = signal.shape
    size = 2 * INNER
    anywhere = pl.BlockSpec(memory_space=pl.ANY)
    inside = pl.BlockSpec(memory_space=pltpu.VMEM)
    square = pltpu.VMEM((OUTER, size, size), BF16)
    return pl.pallas_call(
        conv_kernel,
        in_specs=[inside, anywhere, inside] + [anywhere] * 4,
        out_specs=inside,
        out_shape=jax.ShapeDtypeStruct((length, channels), BF16),
        scratch_shapes=[
            pltpu.VMEM((OUTER, size, channels), F32),
            pltpu.VMEM((OUTER, size, channels), F32),
            square,
            square,
            square,
            square,
            pltpu.SemaphoreType.DMA((5, 8)),
        ],
        compiler_params=pltpu.CompilerParams(vmem_limit_bytes=48 * MIB),
        cost_estimate=pl.CostEstimate(
            flops=12 * OUTER * size * size * channels, bytes_accessed=24 * OUTER * size * size, transcendentals=0
        ),
        name="convolve",
    )(signal, spec, skip, *table)


def project_kernel(queries_ref, mixed_ref, weight_ref, out_ref, gated):
    parts = mixed_ref.shape[0]
    width = mixed_ref.shape[2]

    @pl.when(pl.program_id(0) == 0)
    def _():
        for j in range(parts):
            cols = pl.ds(j * width, width)
            gated[:, cols] = (queries_ref[:, cols].astype(F32) * mixed_ref[j].astype(F32)).astype(BF16)

    out_ref[...] = lax.dot_general(
        gated[...], weight_ref[...], (((1,), (1,)), ((), ())), preferred_element_type=F32
    ).astype(BF16)


def project(queries, mixed, weight):
    rows, width = queries.shape
    features = weight.shape[0]
    tile = 512
    return pl.pallas_call(
        project_kernel,
        grid=(features // tile,),
        in_specs=[
            pl.BlockSpec((rows, width), lambda n: (0, 0)),
            pl.BlockSpec(mixed.shape, lambda n: (0, 0, 0)),
            pl.BlockSpec((tile, width), lambda n: (n, 0)),
        ],
        out_specs=pl.BlockSpec((rows, tile), lambda n: (0, n)),
        out_shape=jax.ShapeDtypeStruct((rows, features), BF16),
        scratch_shapes=[pltpu.VMEM((rows, width), BF16)],
        compiler_params=pltpu.CompilerParams(vmem_limit_bytes=40 * MIB),
        cost_estimate=pl.CostEstimate(
            flops=2 * rows * width * features, bytes_accessed=2 * width * features, transcendentals=0
        ),
        name="project",
    )(queries, mixed, weight)


def on_device(queries, keys_in, values_in, filters, skip_gain, out_weight):
    count = lax.axis_size("ctx")
    rows, width = queries.shape[1:]
    cols = width // count
    table = [jnp.asarray(t) for t in tables()]
    weight = lax.all_gather(out_weight.T, ("dp", "ctx"), axis=0, tiled=True)
    product = product_blocks(keys_in[0], values_in[0], count)
    piece = lax.all_to_all(product, "ctx", split_axis=0, concat_axis=0, tiled=True)
    spec = filter_spectrum(filters, table[0], table[1])
    skip = lax.dynamic_slice_in_dim(skip_gain, lax.axis_index("ctx") * cols, cols).reshape(1, cols)
    mixed = convolve(piece.reshape(count * rows, cols), spec, skip, table)
    returned = lax.all_to_all(mixed.reshape(count, rows, cols), "ctx", split_axis=0, concat_axis=0, tiled=True)
    return project(queries[0], returned, weight)[None]


def solution(mesh):
    in_specs = (
        P("dp", "ctx", None),
        P("dp", "ctx", None),
        P("dp", "ctx", None),
        P("ctx", None),
        P(),
        P(None, ("dp", "ctx")),
    )
    return jax.shard_map(
        on_device, mesh=mesh, in_specs=in_specs, out_specs=P("dp", "ctx", None), check_vma=False
    )
```

```python
import math

import jax
import jax.numpy as jnp
import ml_dtypes
import numpy as np
from jax import lax
from jax.experimental import pallas as pl
from jax.experimental.pallas import tpu as pltpu
from jax.sharding import PartitionSpec as P

F32 = jnp.float32
BF16 = jnp.bfloat16
MIB = 1024 * 1024

OUTER = 32
INNER = 128
CHUNKS = 4


def split_table(table):
    high = table.astype(ml_dtypes.bfloat16)
    low = (table - high.astype(np.float64)).astype(ml_dtypes.bfloat16)
    return high, low


def tables():
    length = OUTER * INNER
    k1 = np.arange(OUTER)[:, None, None]
    k2 = np.arange(INNER)[None, :, None]
    b = np.arange(INNER)[None, None, :]
    theta = 2.0 * math.pi * b * (k1 + 0.25 + OUTER * k2) / length
    cos, sin = np.cos(theta), np.sin(theta)
    top = np.concatenate([cos, sin], axis=2)
    bottom = np.concatenate([-sin, cos], axis=2)
    forward = np.concatenate([top, bottom], axis=1)
    backward = np.swapaxes(forward, 1, 2) / length
    return split_table(forward) + split_table(backward)


def cadd(u, v):
    return (u[0] + v[0], u[1] + v[1])


def csub(u, v):
    return (u[0] - v[0], u[1] - v[1])


def turn(u, angle):
    quarter = round(angle / (math.pi / 2), 9)
    if quarter == int(quarter):
        quarter = int(quarter) % 4
        if quarter == 0:
            return u
        if quarter == 1:
            return (-u[1], u[0])
        if quarter == 2:
            return (-u[0], -u[1])
        return (u[1], -u[0])
    c, s = math.cos(angle), math.sin(angle)
    return (u[0] * c - u[1] * s, u[0] * s + u[1] * c)


def four(u, sign):
    p, q = cadd(u[0], u[2]), csub(u[0], u[2])
    r, t = cadd(u[1], u[3]), csub(u[1], u[3])
    if sign < 0:
        t = (t[1], -t[0])
    else:
        t = (-t[1], t[0])
    return [cadd(p, r), cadd(q, t), csub(p, r), csub(q, t)]


def eight(u, sign):
    even = four(u[0::2], sign)
    odd = four(u[1::2], sign)
    half = math.sqrt(0.5)
    o1, o3 = odd[1], odd[3]
    if sign < 0:
        odd[1] = ((o1[0] + o1[1]) * half, (o1[1] - o1[0]) * half)
        odd[2] = (odd[2][1], -odd[2][0])
        odd[3] = ((o3[1] - o3[0]) * half, (o3[0] + o3[1]) * -half)
    else:
        odd[1] = ((o1[0] - o1[1]) * half, (o1[0] + o1[1]) * half)
        odd[2] = (-odd[2][1], odd[2][0])
        odd[3] = ((o3[0] + o3[1]) * -half, (o3[0] - o3[1]) * half)
    return [cadd(even[i], odd[i]) for i in range(4)] + [csub(even[i], odd[i]) for i in range(4)]


def outer_forward(x):
    c1, s1 = math.cos(math.pi / 8), math.sin(math.pi / 8)
    half = math.sqrt(0.5)
    rows = []
    for r in range(8):
        x0, x1, x2, x3 = x[r], x[r + 8], x[r + 16], x[r + 24]
        x2 = x2 * half
        y0, y1 = (x0 + x2, -x2), (x0 - x2, x2)
        u1, v1 = x1 * c1, x1 * s1
        u3, v3 = x3 * s1, x3 * c1
        p = (u1 + u3, -(v1 + v3))
        d = (u1 - u3, v3 - v1)
        d = (d[1], -d[0])
        rows.append([cadd(y0, p), cadd(y1, d), csub(y0, p), csub(y1, d)])
    out = [None] * OUTER
    for q in range(4):
        column = [turn(rows[r][q], -2.0 * math.pi * r * (q + 0.25) / OUTER) for r in range(8)]
        for k, value in enumerate(eight(column, -1)):
            out[q + 4 * k] = value
    return out


def outer_backward(t):
    columns = []
    for q in range(4):
        g = eight([t[q + 4 * k] for k in range(8)], 1)
        columns.append([turn(g[r], 2.0 * math.pi * r * (q + 0.25) / OUTER) for r in range(8)])
    out = [None] * OUTER
    for r in range(8):
        v = [columns[q][r] for q in range(4)]
        p, s = cadd(v[0], v[2]), csub(v[0], v[2])
        w, d = cadd(v[1], v[3]), csub(v[1], v[3])
        out[r] = p[0] + w[0]
        for j, (re, im) in (
            (1, (s[0] - d[1], s[1] + d[0])),
            (2, csub(p, w)),
            (3, (s[0] + d[1], s[1] - d[0])),
        ):
            c, n = math.cos(math.pi * j / 8), math.sin(math.pi * j / 8)
            out[r + 8 * j] = re * c - im * n
    return out


def split(value):
    high = value.astype(BF16)
    return high, (value - high.astype(F32)).astype(BF16)


def close_dot(high, low, value):
    value_high, value_low = split(value)
    return (
        jnp.dot(high, value_high, preferred_element_type=F32)
        + jnp.dot(high, value_low, preferred_element_type=F32)
        + jnp.dot(low, value_high, preferred_element_type=F32)
    )


def product_kernel(keys_ref, values_ref, out_ref):
    parts, _, cols = out_ref.shape
    for j in range(parts):
        col = pl.ds(j * cols, cols)
        out_ref[j] = (keys_ref[:, col].astype(F32) * values_ref[:, col].astype(F32)).astype(BF16)


def product_blocks(keys, values, parts):
    rows, width = keys.shape
    cols = width // parts
    tile = 64
    return pl.pallas_call(
        product_kernel,
        grid=(rows // tile,),
        in_specs=[pl.BlockSpec((tile, width), lambda j: (j, 0))] * 2,
        out_specs=pl.BlockSpec((parts, tile, cols), lambda j: (0, j, 0)),
        out_shape=jax.ShapeDtypeStruct((parts, rows, cols), BF16),
        cost_estimate=pl.CostEstimate(flops=rows * width, bytes_accessed=6 * rows * width, transcendentals=0),
        name="product",
    )(keys, values)


def spectrum_kernel(filters_ref, high_ref, low_ref, out_ref, taps, high, low, sems):
    chunks = CHUNKS
    step = OUTER // chunks

    def fetch(i):
        part = pl.ds(i * step, step)
        return (
            pltpu.make_async_copy(high_ref.at[part], high.at[part], sems.at[0, i]),
            pltpu.make_async_copy(low_ref.at[part], low.at[part], sems.at[1, i]),
        )

    for i in range(chunks):
        for copy in fetch(i):
            copy.start()
    for a in range(OUTER):
        taps[pl.ds(a * INNER, INNER), :] = filters_ref[:, pl.ds(a * INNER, INNER)].T

    def outer(i, carry):
        base = pl.multiple_of(i * 8, 8)
        x = [taps[pl.ds(a * INNER + base, 8), :] for a in range(OUTER)]
        for k, (re, im) in enumerate(outer_forward(x)):
            out_ref[k, pl.ds(base, 8), :] = re
            out_ref[k, pl.ds(INNER + base, 8), :] = im
        return carry

    lax.fori_loop(0, INNER // 8, outer, 0)
    for i in range(chunks):
        for copy in fetch(i):
            copy.wait()

        def inner(k, carry):
            out_ref[k] = close_dot(high[k], low[k], out_ref[k])
            return carry

        lax.fori_loop(i * step, (i + 1) * step, inner, 0, unroll=step)


def filter_spectrum(filters, high, low):
    channels, length = filters.shape
    lanes = 128
    size = 2 * INNER
    return pl.pallas_call(
        spectrum_kernel,
        grid=(channels // lanes,),
        in_specs=[
            pl.BlockSpec((lanes, length), lambda j: (j, 0)),
            pl.BlockSpec(memory_space=pl.ANY),
            pl.BlockSpec(memory_space=pl.ANY),
        ],
        out_specs=pl.BlockSpec((OUTER, size, lanes), lambda j: (0, 0, j)),
        out_shape=jax.ShapeDtypeStruct((OUTER, size, channels), F32),
        scratch_shapes=[
            pltpu.VMEM((length, lanes), F32),
            pltpu.VMEM((OUTER, size, size), BF16),
            pltpu.VMEM((OUTER, size, size), BF16),
            pltpu.SemaphoreType.DMA((2, CHUNKS)),
        ],
        compiler_params=pltpu.CompilerParams(vmem_limit_bytes=40 * MIB),
        cost_estimate=pl.CostEstimate(
            flops=6 * OUTER * size * size * channels, bytes_accessed=16 * OUTER * size * size, transcendentals=0
        ),
        name="spectrum",
    )(filters, high, low)


def conv_kernel(
    signal_ref, spec_ref, skip_ref, fh_ref, fl_ref, bh_ref, bl_ref, out_ref, work, spec, fh, fl, bh, bl, sems
):
    chunks = CHUNKS
    step = OUTER // chunks
    lanes = 128
    channels = out_ref.shape[1]
    pairs = ((fh_ref, fh), (fl_ref, fl), (spec_ref, spec), (bh_ref, bh), (bl_ref, bl))

    def fetch(i):
        part = pl.ds(i * step, step)
        return [
            pltpu.make_async_copy(source.at[part], target.at[part], sems.at[n, i])
            for n, (source, target) in enumerate(pairs)
        ]

    for i in range(chunks):
        for copy in fetch(i):
            copy.start()

    for c in range(0, channels, lanes):
        col = pl.ds(c, lanes)

        def outer(i, carry):
            base = pl.multiple_of(i * 16, 16)
            rows = [signal_ref[pl.ds(a * INNER + base, 16), col].astype(F32) for a in range(OUTER)]
            for h in range(0, 16, 8):
                for k, (re, im) in enumerate(outer_forward([row[h : h + 8] for row in rows])):
                    work[k, pl.ds(base + h, 8), col] = re
                    work[k, pl.ds(INNER + base + h, 8), col] = im
            return carry

        lax.fori_loop(0, INNER // 16, outer, 0)

    for i in range(chunks):
        for copy in fetch(i):
            copy.wait()

        def inner(k, carry):
            value = close_dot(fh[k], fl[k], work[k])
            re, im = value[:INNER], value[INNER:]
            sre, sim = spec[k, :INNER], spec[k, INNER:]
            mixed = jnp.concatenate([re * sre - im * sim, re * sim + im * sre], axis=0)
            work[k] = close_dot(bh[k], bl[k], mixed)
            return carry

        lax.fori_loop(i * step, (i + 1) * step, inner, 0, unroll=step)

    for c in range(0, channels, lanes):
        col = pl.ds(c, lanes)
        gain = skip_ref[:, col]

        def back(i, carry):
            base = pl.multiple_of(i * 16, 16)
            halves = []
            for h in range(0, 16, 8):
                t = [
                    (work[k, pl.ds(base + h, 8), col], work[k, pl.ds(INNER + base + h, 8), col])
                    for k in range(OUTER)
                ]
                halves.append(outer_backward(t))
            for a in range(OUTER):
                rows = pl.ds(a * INNER + base, 16)
                causal = jnp.concatenate([halves[0][a], halves[1][a]], axis=0)
                out_ref[rows, col] = (causal + gain * signal_ref[rows, col].astype(F32)).astype(BF16)
            return carry

        lax.fori_loop(0, INNER // 16, back, 0)


def convolve(signal, spec, skip, table):
    length, channels = signal.shape
    size = 2 * INNER
    anywhere = pl.BlockSpec(memory_space=pl.ANY)
    inside = pl.BlockSpec(memory_space=pltpu.VMEM)
    square = pltpu.VMEM((OUTER, size, size), BF16)
    return pl.pallas_call(
        conv_kernel,
        in_specs=[inside, anywhere, inside] + [anywhere] * 4,
        out_specs=inside,
        out_shape=jax.ShapeDtypeStruct((length, channels), BF16),
        scratch_shapes=[
            pltpu.VMEM((OUTER, size, channels), F32),
            pltpu.VMEM((OUTER, size, channels), F32),
            square,
            square,
            square,
            square,
            pltpu.SemaphoreType.DMA((5, CHUNKS)),
        ],
        compiler_params=pltpu.CompilerParams(vmem_limit_bytes=48 * MIB),
        cost_estimate=pl.CostEstimate(
            flops=12 * OUTER * size * size * channels, bytes_accessed=24 * OUTER * size * size, transcendentals=0
        ),
        name="convolve",
    )(signal, spec, skip, *table)


def project_kernel(queries_ref, mixed_ref, weight_ref, out_ref, gated):
    parts = mixed_ref.shape[0]
    width = mixed_ref.shape[2]

    @pl.when(pl.program_id(0) == 0)
    def _():
        for j in range(parts):
            cols = pl.ds(j * width, width)
            gated[:, cols] = (queries_ref[:, cols].astype(F32) * mixed_ref[j].astype(F32)).astype(BF16)

    out_ref[...] = lax.dot_general(
        gated[...], weight_ref[...], (((1,), (1,)), ((), ())), preferred_element_type=F32
    ).astype(BF16)


def project(queries, mixed, weight):
    rows, width = queries.shape
    features = weight.shape[0]
    tile = 512
    return pl.pallas_call(
        project_kernel,
        grid=(features // tile,),
        in_specs=[
            pl.BlockSpec((rows, width), lambda n: (0, 0)),
            pl.BlockSpec(mixed.shape, lambda n: (0, 0, 0)),
            pl.BlockSpec((tile, width), lambda n: (n, 0)),
        ],
        out_specs=pl.BlockSpec((rows, tile), lambda n: (0, n)),
        out_shape=jax.ShapeDtypeStruct((rows, features), BF16),
        scratch_shapes=[pltpu.VMEM((rows, width), BF16)],
        compiler_params=pltpu.CompilerParams(vmem_limit_bytes=40 * MIB),
        cost_estimate=pl.CostEstimate(
            flops=2 * rows * width * features, bytes_accessed=2 * width * features, transcendentals=0
        ),
        name="project",
    )(queries, mixed, weight)


def on_device(queries, keys_in, values_in, filters, skip_gain, out_weight):
    count = lax.axis_size("ctx")
    rows, width = queries.shape[1:]
    cols = width // count
    table = [jnp.asarray(t) for t in tables()]
    weight = lax.all_gather(out_weight.T, ("dp", "ctx"), axis=0, tiled=True)
    product = product_blocks(keys_in[0], values_in[0], count)
    piece = lax.all_to_all(product, "ctx", split_axis=0, concat_axis=0, tiled=True)
    spec = filter_spectrum(filters, table[0], table[1])
    skip = lax.dynamic_slice_in_dim(skip_gain, lax.axis_index("ctx") * cols, cols).reshape(1, cols)
    mixed = convolve(piece.reshape(count * rows, cols), spec, skip, table)
    returned = lax.all_to_all(mixed.reshape(count, rows, cols), "ctx", split_axis=0, concat_axis=0, tiled=True)
    return project(queries[0], returned, weight)[None]


def solution(mesh):
    in_specs = (
        P("dp", "ctx", None),
        P("dp", "ctx", None),
        P("dp", "ctx", None),
        P("ctx", None),
        P(),
        P(None, ("dp", "ctx")),
    )
    return jax.shard_map(
        on_device, mesh=mesh, in_specs=in_specs, out_specs=P("dp", "ctx", None), check_vma=False
    )
```

```python
import math

import jax
import jax.numpy as jnp
import ml_dtypes
import numpy as np
from jax import lax
from jax.experimental import pallas as pl
from jax.experimental.pallas import tpu as pltpu
from jax.sharding import Mesh
from jax.sharding import PartitionSpec as P

F32 = jnp.float32
BF16 = jnp.bfloat16
MIB = 1024 * 1024

OUTER = 32
INNER = 128
CHUNKS = 4


def split_table(table):
    high = table.astype(ml_dtypes.bfloat16)
    low = (table - high.astype(np.float64)).astype(ml_dtypes.bfloat16)
    return high, low


def tables():
    length = OUTER * INNER
    k1 = np.arange(OUTER)[:, None, None]
    k2 = np.arange(INNER)[None, :, None]
    b = np.arange(INNER)[None, None, :]
    theta = 2.0 * math.pi * b * (k1 + 0.25 + OUTER * k2) / length
    cos, sin = np.cos(theta), np.sin(theta)
    top = np.concatenate([cos, sin], axis=2)
    bottom = np.concatenate([-sin, cos], axis=2)
    forward = np.concatenate([top, bottom], axis=1)
    backward = np.swapaxes(forward, 1, 2) / length
    return split_table(forward) + split_table(backward)


def cadd(u, v):
    return (u[0] + v[0], u[1] + v[1])


def csub(u, v):
    return (u[0] - v[0], u[1] - v[1])


def turn(u, angle):
    quarter = round(angle / (math.pi / 2), 9)
    if quarter == int(quarter):
        quarter = int(quarter) % 4
        if quarter == 0:
            return u
        if quarter == 1:
            return (-u[1], u[0])
        if quarter == 2:
            return (-u[0], -u[1])
        return (u[1], -u[0])
    c, s = math.cos(angle), math.sin(angle)
    return (u[0] * c - u[1] * s, u[0] * s + u[1] * c)


def four(u, sign):
    p, q = cadd(u[0], u[2]), csub(u[0], u[2])
    r, t = cadd(u[1], u[3]), csub(u[1], u[3])
    if sign < 0:
        t = (t[1], -t[0])
    else:
        t = (-t[1], t[0])
    return [cadd(p, r), cadd(q, t), csub(p, r), csub(q, t)]


def eight(u, sign):
    even = four(u[0::2], sign)
    odd = four(u[1::2], sign)
    half = math.sqrt(0.5)
    o1, o3 = odd[1], odd[3]
    if sign < 0:
        odd[1] = ((o1[0] + o1[1]) * half, (o1[1] - o1[0]) * half)
        odd[2] = (odd[2][1], -odd[2][0])
        odd[3] = ((o3[1] - o3[0]) * half, (o3[0] + o3[1]) * -half)
    else:
        odd[1] = ((o1[0] - o1[1]) * half, (o1[0] + o1[1]) * half)
        odd[2] = (-odd[2][1], odd[2][0])
        odd[3] = ((o3[0] + o3[1]) * -half, (o3[0] - o3[1]) * half)
    return [cadd(even[i], odd[i]) for i in range(4)] + [csub(even[i], odd[i]) for i in range(4)]


def outer_forward(x):
    c1, s1 = math.cos(math.pi / 8), math.sin(math.pi / 8)
    half = math.sqrt(0.5)
    rows = []
    for r in range(8):
        x0, x1, x2, x3 = x[r], x[r + 8], x[r + 16], x[r + 24]
        x2 = x2 * half
        y0, y1 = (x0 + x2, -x2), (x0 - x2, x2)
        u1, v1 = x1 * c1, x1 * s1
        u3, v3 = x3 * s1, x3 * c1
        p = (u1 + u3, -(v1 + v3))
        d = (u1 - u3, v3 - v1)
        d = (d[1], -d[0])
        rows.append([cadd(y0, p), cadd(y1, d), csub(y0, p), csub(y1, d)])
    out = [None] * OUTER
    for q in range(4):
        column = [turn(rows[r][q], -2.0 * math.pi * r * (q + 0.25) / OUTER) for r in range(8)]
        for k, value in enumerate(eight(column, -1)):
            out[q + 4 * k] = value
    return out


def outer_backward(t):
    columns = []
    for q in range(4):
        g = eight([t[q + 4 * k] for k in range(8)], 1)
        columns.append([turn(g[r], 2.0 * math.pi * r * (q + 0.25) / OUTER) for r in range(8)])
    out = [None] * OUTER
    for r in range(8):
        v = [columns[q][r] for q in range(4)]
        p, s = cadd(v[0], v[2]), csub(v[0], v[2])
        w, d = cadd(v[1], v[3]), csub(v[1], v[3])
        out[r] = p[0] + w[0]
        for j, (re, im) in (
            (1, (s[0] - d[1], s[1] + d[0])),
            (2, csub(p, w)),
            (3, (s[0] + d[1], s[1] - d[0])),
        ):
            c, n = math.cos(math.pi * j / 8), math.sin(math.pi * j / 8)
            out[r + 8 * j] = re * c - im * n
    return out


def split(value):
    high = value.astype(BF16)
    return high, (value - high.astype(F32)).astype(BF16)


def close_dot(high, low, value):
    value_high, value_low = split(value)
    return (
        jnp.dot(high, value_high, preferred_element_type=F32)
        + jnp.dot(high, value_low, preferred_element_type=F32)
        + jnp.dot(low, value_high, preferred_element_type=F32)
    )


def product_kernel(keys_ref, values_ref, out_ref):
    parts, _, cols = out_ref.shape
    for j in range(parts):
        col = pl.ds(j * cols, cols)
        out_ref[j] = (keys_ref[:, col].astype(F32) * values_ref[:, col].astype(F32)).astype(BF16)


def product_blocks(keys, values, parts):
    rows, width = keys.shape
    cols = width // parts
    tile = 64
    return pl.pallas_call(
        product_kernel,
        grid=(rows // tile,),
        in_specs=[pl.BlockSpec((tile, width), lambda j: (j, 0))] * 2,
        out_specs=pl.BlockSpec((parts, tile, cols), lambda j: (0, j, 0)),
        out_shape=jax.ShapeDtypeStruct((parts, rows, cols), BF16),
        cost_estimate=pl.CostEstimate(flops=rows * width, bytes_accessed=6 * rows * width, transcendentals=0),
        name="product",
    )(keys, values)


def spectrum_kernel(filters_ref, high_ref, low_ref, out_ref, taps, high, low, sems):
    chunks = CHUNKS
    step = OUTER // chunks

    def fetch(i):
        part = pl.ds(i * step, step)
        return (
            pltpu.make_async_copy(high_ref.at[part], high.at[part], sems.at[0, i]),
            pltpu.make_async_copy(low_ref.at[part], low.at[part], sems.at[1, i]),
        )

    for i in range(chunks):
        for copy in fetch(i):
            copy.start()
    for a in range(OUTER):
        taps[pl.ds(a * INNER, INNER), :] = filters_ref[:, pl.ds(a * INNER, INNER)].T

    def outer(i, carry):
        base = pl.multiple_of(i * 8, 8)
        x = [taps[pl.ds(a * INNER + base, 8), :] for a in range(OUTER)]
        for k, (re, im) in enumerate(outer_forward(x)):
            out_ref[k, pl.ds(base, 8), :] = re
            out_ref[k, pl.ds(INNER + base, 8), :] = im
        return carry

    lax.fori_loop(0, INNER // 8, outer, 0)
    for i in range(chunks):
        for copy in fetch(i):
            copy.wait()

        def inner(k, carry):
            out_ref[k] = close_dot(high[k], low[k], out_ref[k])
            return carry

        lax.fori_loop(i * step, (i + 1) * step, inner, 0, unroll=step)


def filter_spectrum(filters, high, low):
    channels, length = filters.shape
    lanes = 128
    size = 2 * INNER
    return pl.pallas_call(
        spectrum_kernel,
        grid=(channels // lanes,),
        in_specs=[
            pl.BlockSpec((lanes, length), lambda j: (j, 0)),
            pl.BlockSpec(memory_space=pl.ANY),
            pl.BlockSpec(memory_space=pl.ANY),
        ],
        out_specs=pl.BlockSpec((OUTER, size, lanes), lambda j: (0, 0, j)),
        out_shape=jax.ShapeDtypeStruct((OUTER, size, channels), F32),
        scratch_shapes=[
            pltpu.VMEM((length, lanes), F32),
            pltpu.VMEM((OUTER, size, size), BF16),
            pltpu.VMEM((OUTER, size, size), BF16),
            pltpu.SemaphoreType.DMA((2, CHUNKS)),
        ],
        compiler_params=pltpu.CompilerParams(vmem_limit_bytes=40 * MIB),
        cost_estimate=pl.CostEstimate(
            flops=6 * OUTER * size * size * channels, bytes_accessed=16 * OUTER * size * size, transcendentals=0
        ),
        name="spectrum",
    )(filters, high, low)


def conv_kernel(
    signal_ref, spec_ref, skip_ref, fh_ref, fl_ref, bh_ref, bl_ref, out_ref, work, spec, fh, fl, bh, bl, sems
):
    chunks = CHUNKS
    step = OUTER // chunks
    lanes = 128
    channels = out_ref.shape[1]
    pairs = ((fh_ref, fh), (fl_ref, fl), (spec_ref, spec), (bh_ref, bh), (bl_ref, bl))

    def fetch(i):
        part = pl.ds(i * step, step)
        return [
            pltpu.make_async_copy(source.at[part], target.at[part], sems.at[n, i])
            for n, (source, target) in enumerate(pairs)
        ]

    for i in range(chunks):
        for copy in fetch(i):
            copy.start()

    for c in range(0, channels, lanes):
        col = pl.ds(c, lanes)

        def outer(i, carry):
            base = pl.multiple_of(i * 16, 16)
            rows = [signal_ref[pl.ds(a * INNER + base, 16), col].astype(F32) for a in range(OUTER)]
            for h in range(0, 16, 8):
                for k, (re, im) in enumerate(outer_forward([row[h : h + 8] for row in rows])):
                    work[k, pl.ds(base + h, 8), col] = re
                    work[k, pl.ds(INNER + base + h, 8), col] = im
            return carry

        lax.fori_loop(0, INNER // 16, outer, 0)

    for i in range(chunks):
        for copy in fetch(i):
            copy.wait()

        def inner(k, carry):
            value = close_dot(fh[k], fl[k], work[k])
            re, im = value[:INNER], value[INNER:]
            sre, sim = spec[k, :INNER], spec[k, INNER:]
            mixed = jnp.concatenate([re * sre - im * sim, re * sim + im * sre], axis=0)
            work[k] = close_dot(bh[k], bl[k], mixed)
            return carry

        lax.fori_loop(i * step, (i + 1) * step, inner, 0, unroll=step)

    for c in range(0, channels, lanes):
        col = pl.ds(c, lanes)
        gain = skip_ref[:, col]

        def back(i, carry):
            base = pl.multiple_of(i * 16, 16)
            halves = []
            for h in range(0, 16, 8):
                t = [
                    (work[k, pl.ds(base + h, 8), col], work[k, pl.ds(INNER + base + h, 8), col])
                    for k in range(OUTER)
                ]
                halves.append(outer_backward(t))
            for a in range(OUTER):
                rows = pl.ds(a * INNER + base, 16)
                causal = jnp.concatenate([halves[0][a], halves[1][a]], axis=0)
                out_ref[rows, col] = (causal + gain * signal_ref[rows, col].astype(F32)).astype(BF16)
            return carry

        lax.fori_loop(0, INNER // 16, back, 0)


def convolve(signal, spec, skip, table):
    length, channels = signal.shape
    size = 2 * INNER
    anywhere = pl.BlockSpec(memory_space=pl.ANY)
    inside = pl.BlockSpec(memory_space=pltpu.VMEM)
    square = pltpu.VMEM((OUTER, size, size), BF16)
    return pl.pallas_call(
        conv_kernel,
        in_specs=[inside, anywhere, inside] + [anywhere] * 4,
        out_specs=inside,
        out_shape=jax.ShapeDtypeStruct((length, channels), BF16),
        scratch_shapes=[
            pltpu.VMEM((OUTER, size, channels), F32),
            pltpu.VMEM((OUTER, size, channels), F32),
            square,
            square,
            square,
            square,
            pltpu.SemaphoreType.DMA((5, CHUNKS)),
        ],
        compiler_params=pltpu.CompilerParams(vmem_limit_bytes=48 * MIB),
        cost_estimate=pl.CostEstimate(
            flops=12 * OUTER * size * size * channels, bytes_accessed=24 * OUTER * size * size, transcendentals=0
        ),
        name="convolve",
    )(signal, spec, skip, *table)


def project_kernel(place_ref, queries_ref, mixed_ref, weight_ref, *rest):
    tiles = group_tiles(rest[:-4])
    out_ref, gated, held, sems = rest[-4:]
    parts, _, width = mixed_ref.shape
    depth = weight_ref.shape[1]
    step = pl.program_id(0)
    half = held.shape[1] // 2

    def copies(i):
        slot = held.at[i % 2]
        if len(tiles[i]) == 1:
            return [pltpu.make_async_copy(tiles[i][0], slot, sems.at[i % 2, 0])]
        return [
            pltpu.make_async_copy(part, slot.at[pl.ds(h * half, half)], sems.at[i % 2, h])
            for h, part in enumerate(tiles[i])
        ]

    count = len(tiles)

    @pl.when(step == 0)
    def _():
        for copy in copies(0):
            copy.start()
        for j in range(parts):
            cols = pl.ds(j * width, width)
            gated[:, cols] = (queries_ref[:, cols].astype(F32) * mixed_ref[j].astype(F32)).astype(BF16)

    for i in range(count):

        @pl.when(step == i)
        def _():
            if i + 1 < count:
                for copy in copies(i + 1):
                    copy.start()
            for copy in copies(i):
                copy.wait()
            dims = (((1,), (1,)), ((), ()))
            first = lax.dot_general(gated[:, :depth], weight_ref[...], dims, preferred_element_type=F32)
            second = lax.dot_general(gated[:, depth:], held[i % 2], dims, preferred_element_type=F32)
            out_ref[...] = (first + second).astype(BF16)


def group_tiles(refs):
    groups = []
    for base in (0, 5):
        own, back, ahead, far_low, far_high = refs[base : base + 5]
        groups += [(own,), (back,), (ahead,), (far_low, far_high)]
    return groups


def project(queries, mixed, weight, tiles, place):
    rows, width = queries.shape
    features, depth = weight.shape
    tile, rest = tiles[0].shape
    return pl.pallas_call(
        project_kernel,
        grid_spec=pltpu.PrefetchScalarGridSpec(
            num_scalar_prefetch=1,
            grid=(features // tile,),
            in_specs=[
                pl.BlockSpec((rows, width), lambda n, place: (0, 0)),
                pl.BlockSpec(mixed.shape, lambda n, place: (0, 0, 0)),
                pl.BlockSpec((tile, depth), lambda n, place: (place[n], 0)),
            ]
            + [pl.BlockSpec(memory_space=pl.ANY)] * len(tiles),
            out_specs=pl.BlockSpec((rows, tile), lambda n, place: (0, place[n])),
            scratch_shapes=[
                pltpu.VMEM((rows, width), BF16),
                pltpu.VMEM((2, tile, rest), BF16),
                pltpu.SemaphoreType.DMA((2, 2)),
            ],
        ),
        out_shape=jax.ShapeDtypeStruct((rows, features), BF16),
        compiler_params=pltpu.CompilerParams(vmem_limit_bytes=40 * MIB),
        cost_estimate=pl.CostEstimate(
            flops=2 * rows * width * features, bytes_accessed=2 * width * features, transcendentals=0
        ),
        name="project",
    )(place, queries, mixed, weight, *tiles)


def around(block, axis):
    size = lax.axis_size(axis)
    half = block.shape[0] // 2
    up = [(i, (i + 1) % size) for i in range(size)]
    down = [(i, (i - 1) % size) for i in range(size)]
    back = lax.ppermute(block, axis, up)
    ahead = lax.ppermute(block, axis, down)
    far_low = lax.ppermute(back[:half], axis, up)
    far_high = lax.ppermute(ahead[half:], axis, down)
    return block, back, ahead, far_low, far_high


def gather_ring(block, axis):
    size = lax.axis_size(axis)
    me = lax.axis_index(axis)
    rows = block.shape[0]
    own, back, ahead, far_low, far_high = around(block, axis)
    whole = jnp.zeros((size * rows, block.shape[1]), block.dtype)
    for piece, shift, offset in ((own, 0, 0), (back, -1, 0), (ahead, 1, 0), (far_low, 2, 0), (far_high, 2, rows // 2)):
        start = (me + shift + size) % size * rows + offset
        whole = lax.dynamic_update_slice_in_dim(whole, piece, start, 0)
    return whole


def gather_tiles(block):
    plane = gather_ring(gather_ring(block, "z"), "x")
    mine = around(plane, "y")
    others = [lax.ppermute(piece, "core", [(0, 1), (1, 0)]) for piece in mine]
    y, core = lax.axis_index("y"), lax.axis_index("core")
    count = lax.axis_size("y")
    place = [(y + shift + count) % count * 2 + c for c in (core, 1 - core) for shift in (0, -1, 1, 2)]
    return list(mine) + others, jnp.stack(place).astype(jnp.int32)


def on_device(queries, keys_in, values_in, filters, skip_gain, out_weight):
    ctx = ("x", "z")
    count = lax.axis_size(ctx)
    rows, width = queries.shape[1:]
    cols = width // count
    depth = width // 2
    table = [jnp.asarray(t) for t in tables()]
    turned = out_weight.T
    weight = lax.all_gather(turned[:, :depth], ("y", "core", "x", "z"), axis=0, tiled=True)
    tiles, place = gather_tiles(turned[:, depth:])
    product = product_blocks(keys_in[0], values_in[0], count)
    piece = lax.all_to_all(product, ctx, split_axis=0, concat_axis=0, tiled=True)
    spec = filter_spectrum(filters, table[0], table[1])
    skip = lax.dynamic_slice_in_dim(skip_gain, lax.axis_index(ctx) * cols, cols).reshape(1, cols)
    mixed = convolve(piece.reshape(count * rows, cols), spec, skip, table)
    returned = lax.all_to_all(mixed.reshape(count, rows, cols), ctx, split_axis=0, concat_axis=0, tiled=True)
    return project(queries[0], returned, weight, tiles, place)[None]


def solution(mesh):
    chips = Mesh(mesh.devices.reshape(4, 2, 4, 4), ("y", "core", "x", "z"))
    dp, ctx = ("y", "core"), ("x", "z")
    in_specs = (
        P(dp, ctx, None),
        P(dp, ctx, None),
        P(dp, ctx, None),
        P(ctx, None),
        P(),
        P(None, dp + ctx),
    )
    return jax.shard_map(
        on_device, mesh=chips, in_specs=in_specs, out_specs=P(dp, ctx, None), check_vma=False
    )
```

```python
import math

import jax
import jax.numpy as jnp
import ml_dtypes
import numpy as np
from jax import lax
from jax.experimental import pallas as pl
from jax.experimental.pallas import tpu as pltpu
from jax.sharding import PartitionSpec as P

F32 = jnp.float32
BF16 = jnp.bfloat16
MIB = 1024 * 1024

OUTER = 32
INNER = 128
CHUNKS = 4


def split_table(table):
    high = table.astype(ml_dtypes.bfloat16)
    low = (table - high.astype(np.float64)).astype(ml_dtypes.bfloat16)
    return high, low


def tables():
    length = OUTER * INNER
    k1 = np.arange(OUTER)[:, None, None]
    k2 = np.arange(INNER)[None, :, None]
    b = np.arange(INNER)[None, None, :]
    theta = 2.0 * math.pi * b * (k1 + 0.25 + OUTER * k2) / length
    cos, sin = np.cos(theta), np.sin(theta)
    top = np.concatenate([cos, sin], axis=2)
    bottom = np.concatenate([-sin, cos], axis=2)
    forward = np.concatenate([top, bottom], axis=1)
    backward = np.swapaxes(forward, 1, 2) / length
    return split_table(forward) + split_table(backward)


def cadd(u, v):
    return (u[0] + v[0], u[1] + v[1])


def csub(u, v):
    return (u[0] - v[0], u[1] - v[1])


def turn(u, angle):
    quarter = round(angle / (math.pi / 2), 9)
    if quarter == int(quarter):
        quarter = int(quarter) % 4
        if quarter == 0:
            return u
        if quarter == 1:
            return (-u[1], u[0])
        if quarter == 2:
            return (-u[0], -u[1])
        return (u[1], -u[0])
    c, s = math.cos(angle), math.sin(angle)
    return (u[0] * c - u[1] * s, u[0] * s + u[1] * c)


def four(u, sign):
    p, q = cadd(u[0], u[2]), csub(u[0], u[2])
    r, t = cadd(u[1], u[3]), csub(u[1], u[3])
    if sign < 0:
        t = (t[1], -t[0])
    else:
        t = (-t[1], t[0])
    return [cadd(p, r), cadd(q, t), csub(p, r), csub(q, t)]


def eight(u, sign):
    even = four(u[0::2], sign)
    odd = four(u[1::2], sign)
    half = math.sqrt(0.5)
    o1, o3 = odd[1], odd[3]
    if sign < 0:
        odd[1] = ((o1[0] + o1[1]) * half, (o1[1] - o1[0]) * half)
        odd[2] = (odd[2][1], -odd[2][0])
        odd[3] = ((o3[1] - o3[0]) * half, (o3[0] + o3[1]) * -half)
    else:
        odd[1] = ((o1[0] - o1[1]) * half, (o1[0] + o1[1]) * half)
        odd[2] = (-odd[2][1], odd[2][0])
        odd[3] = ((o3[0] + o3[1]) * -half, (o3[0] - o3[1]) * half)
    return [cadd(even[i], odd[i]) for i in range(4)] + [csub(even[i], odd[i]) for i in range(4)]


def outer_forward(x):
    c1, s1 = math.cos(math.pi / 8), math.sin(math.pi / 8)
    half = math.sqrt(0.5)
    rows = []
    for r in range(8):
        x0, x1, x2, x3 = x[r], x[r + 8], x[r + 16], x[r + 24]
        x2 = x2 * half
        y0, y1 = (x0 + x2, -x2), (x0 - x2, x2)
        u1, v1 = x1 * c1, x1 * s1
        u3, v3 = x3 * s1, x3 * c1
        p = (u1 + u3, -(v1 + v3))
        d = (u1 - u3, v3 - v1)
        d = (d[1], -d[0])
        rows.append([cadd(y0, p), cadd(y1, d), csub(y0, p), csub(y1, d)])
    out = [None] * OUTER
    for q in range(4):
        column = [turn(rows[r][q], -2.0 * math.pi * r * (q + 0.25) / OUTER) for r in range(8)]
        for k, value in enumerate(eight(column, -1)):
            out[q + 4 * k] = value
    return out


def outer_backward(t):
    columns = []
    for q in range(4):
        g = eight([t[q + 4 * k] for k in range(8)], 1)
        columns.append([turn(g[r], 2.0 * math.pi * r * (q + 0.25) / OUTER) for r in range(8)])
    out = [None] * OUTER
    for r in range(8):
        v = [columns[q][r] for q in range(4)]
        p, s = cadd(v[0], v[2]), csub(v[0], v[2])
        w, d = cadd(v[1], v[3]), csub(v[1], v[3])
        out[r] = p[0] + w[0]
        for j, (re, im) in (
            (1, (s[0] - d[1], s[1] + d[0])),
            (2, csub(p, w)),
            (3, (s[0] + d[1], s[1] - d[0])),
        ):
            c, n = math.cos(math.pi * j / 8), math.sin(math.pi * j / 8)
            out[r + 8 * j] = re * c - im * n
    return out


def split(value):
    high = value.astype(BF16)
    return high, (value - high.astype(F32)).astype(BF16)


def close_dot(high, low, value):
    value_high, value_low = split(value)
    return (
        jnp.dot(high, value_high, preferred_element_type=F32)
        + jnp.dot(high, value_low, preferred_element_type=F32)
        + jnp.dot(low, value_high, preferred_element_type=F32)
    )


def product_kernel(keys_ref, values_ref, out_ref):
    parts, _, cols = out_ref.shape
    for j in range(parts):
        col = pl.ds(j * cols, cols)
        out_ref[j] = (keys_ref[:, col].astype(F32) * values_ref[:, col].astype(F32)).astype(BF16)


def product_blocks(keys, values, parts):
    rows, width = keys.shape
    cols = width // parts
    tile = 64
    return pl.pallas_call(
        product_kernel,
        grid=(rows // tile,),
        in_specs=[pl.BlockSpec((tile, width), lambda j: (j, 0))] * 2,
        out_specs=pl.BlockSpec((parts, tile, cols), lambda j: (0, j, 0)),
        out_shape=jax.ShapeDtypeStruct((parts, rows, cols), BF16),
        cost_estimate=pl.CostEstimate(flops=rows * width, bytes_accessed=6 * rows * width, transcendentals=0),
        name="product",
    )(keys, values)


def spectrum_kernel(filters_ref, high_ref, low_ref, out_ref, taps, high, low, sems):
    chunks = CHUNKS
    step = OUTER // chunks

    def fetch(i):
        part = pl.ds(i * step, step)
        return (
            pltpu.make_async_copy(high_ref.at[part], high.at[part], sems.at[0, i]),
            pltpu.make_async_copy(low_ref.at[part], low.at[part], sems.at[1, i]),
        )

    for i in range(chunks):
        for copy in fetch(i):
            copy.start()
    for a in range(OUTER):
        taps[pl.ds(a * INNER, INNER), :] = filters_ref[:, pl.ds(a * INNER, INNER)].T

    def outer(i, carry):
        base = pl.multiple_of(i * 8, 8)
        x = [taps[pl.ds(a * INNER + base, 8), :] for a in range(OUTER)]
        for k, (re, im) in enumerate(outer_forward(x)):
            out_ref[k, pl.ds(base, 8), :] = re
            out_ref[k, pl.ds(INNER + base, 8), :] = im
        return carry

    lax.fori_loop(0, INNER // 8, outer, 0)
    for i in range(chunks):
        for copy in fetch(i):
            copy.wait()

        def inner(k, carry):
            out_ref[k] = close_dot(high[k], low[k], out_ref[k])
            return carry

        lax.fori_loop(i * step, (i + 1) * step, inner, 0, unroll=step)


def filter_spectrum(filters, high, low):
    channels, length = filters.shape
    lanes = 128
    size = 2 * INNER
    return pl.pallas_call(
        spectrum_kernel,
        grid=(channels // lanes,),
        in_specs=[
            pl.BlockSpec((lanes, length), lambda j: (j, 0)),
            pl.BlockSpec(memory_space=pl.ANY),
            pl.BlockSpec(memory_space=pl.ANY),
        ],
        out_specs=pl.BlockSpec((OUTER, size, lanes), lambda j: (0, 0, j)),
        out_shape=jax.ShapeDtypeStruct((OUTER, size, channels), F32),
        scratch_shapes=[
            pltpu.VMEM((length, lanes), F32),
            pltpu.VMEM((OUTER, size, size), BF16),
            pltpu.VMEM((OUTER, size, size), BF16),
            pltpu.SemaphoreType.DMA((2, CHUNKS)),
        ],
        compiler_params=pltpu.CompilerParams(vmem_limit_bytes=40 * MIB),
        cost_estimate=pl.CostEstimate(
            flops=6 * OUTER * size * size * channels, bytes_accessed=16 * OUTER * size * size, transcendentals=0
        ),
        name="spectrum",
    )(filters, high, low)


def conv_kernel(
    signal_ref, spec_ref, skip_ref, fh_ref, fl_ref, bh_ref, bl_ref, out_ref, work, spec, fh, fl, bh, bl, sems
):
    chunks = CHUNKS
    step = OUTER // chunks
    lanes = 128
    channels = out_ref.shape[1]
    pairs = ((fh_ref, fh), (fl_ref, fl), (spec_ref, spec), (bh_ref, bh), (bl_ref, bl))

    def fetch(i):
        part = pl.ds(i * step, step)
        return [
            pltpu.make_async_copy(source.at[part], target.at[part], sems.at[n, i])
            for n, (source, target) in enumerate(pairs)
        ]

    for i in range(chunks):
        for copy in fetch(i):
            copy.start()

    for c in range(0, channels, lanes):
        col = pl.ds(c, lanes)

        def outer(i, carry):
            base = pl.multiple_of(i * 16, 16)
            rows = [signal_ref[pl.ds(a * INNER + base, 16), col].astype(F32) for a in range(OUTER)]
            for h in range(0, 16, 8):
                for k, (re, im) in enumerate(outer_forward([row[h : h + 8] for row in rows])):
                    work[k, pl.ds(base + h, 8), col] = re
                    work[k, pl.ds(INNER + base + h, 8), col] = im
            return carry

        lax.fori_loop(0, INNER // 16, outer, 0)

    for i in range(chunks):
        for copy in fetch(i):
            copy.wait()

        def inner(k, carry):
            value = close_dot(fh[k], fl[k], work[k])
            re, im = value[:INNER], value[INNER:]
            sre, sim = spec[k, :INNER], spec[k, INNER:]
            mixed = jnp.concatenate([re * sre - im * sim, re * sim + im * sre], axis=0)
            work[k] = close_dot(bh[k], bl[k], mixed)
            return carry

        lax.fori_loop(i * step, (i + 1) * step, inner, 0, unroll=step)

    for c in range(0, channels, lanes):
        col = pl.ds(c, lanes)
        gain = skip_ref[:, col]

        def back(i, carry):
            base = pl.multiple_of(i * 16, 16)
            halves = []
            for h in range(0, 16, 8):
                t = [
                    (work[k, pl.ds(base + h, 8), col], work[k, pl.ds(INNER + base + h, 8), col])
                    for k in range(OUTER)
                ]
                halves.append(outer_backward(t))
            for a in range(OUTER):
                rows = pl.ds(a * INNER + base, 16)
                causal = jnp.concatenate([halves[0][a], halves[1][a]], axis=0)
                out_ref[rows, col] = (causal + gain * signal_ref[rows, col].astype(F32)).astype(BF16)
            return carry

        lax.fori_loop(0, INNER // 16, back, 0)


def convolve(signal, spec, skip, table):
    length, channels = signal.shape
    size = 2 * INNER
    anywhere = pl.BlockSpec(memory_space=pl.ANY)
    inside = pl.BlockSpec(memory_space=pltpu.VMEM)
    square = pltpu.VMEM((OUTER, size, size), BF16)
    return pl.pallas_call(
        conv_kernel,
        in_specs=[inside, anywhere, inside] + [anywhere] * 4,
        out_specs=inside,
        out_shape=jax.ShapeDtypeStruct((length, channels), BF16),
        scratch_shapes=[
            pltpu.VMEM((OUTER, size, channels), F32),
            pltpu.VMEM((OUTER, size, channels), F32),
            square,
            square,
            square,
            square,
            pltpu.SemaphoreType.DMA((5, CHUNKS)),
        ],
        compiler_params=pltpu.CompilerParams(vmem_limit_bytes=48 * MIB),
        cost_estimate=pl.CostEstimate(
            flops=12 * OUTER * size * size * channels, bytes_accessed=24 * OUTER * size * size, transcendentals=0
        ),
        name="convolve",
    )(signal, spec, skip, *table)


def gate_kernel(queries_ref, mixed_ref, out_ref):
    parts, _, width = mixed_ref.shape
    for j in range(parts):
        cols = pl.ds(j * width, width)
        out_ref[:, cols] = (queries_ref[:, cols].astype(F32) * mixed_ref[j].astype(F32)).astype(BF16)


def gate(queries, mixed):
    rows, width = queries.shape
    parts, _, cols = mixed.shape
    tile = 64
    return pl.pallas_call(
        gate_kernel,
        grid=(rows // tile,),
        in_specs=[
            pl.BlockSpec((tile, width), lambda j: (j, 0)),
            pl.BlockSpec((parts, tile, cols), lambda j: (0, j, 0)),
        ],
        out_specs=pl.BlockSpec((tile, width), lambda j: (j, 0)),
        out_shape=jax.ShapeDtypeStruct((rows, width), BF16),
        cost_estimate=pl.CostEstimate(flops=rows * width, bytes_accessed=6 * rows * width, transcendentals=0),
        name="gate",
    )(queries, mixed)


def project_kernel(gated_ref, weight_ref, out_ref):
    out_ref[...] = lax.dot_general(
        gated_ref[...], weight_ref[...], (((1,), (1,)), ((), ())), preferred_element_type=F32
    ).astype(BF16)


def project(gated, weight):
    rows, width = gated.shape
    features = weight.shape[0]
    tile = 1024
    return pl.pallas_call(
        project_kernel,
        grid=(features // tile,),
        in_specs=[
            pl.BlockSpec((rows, width), lambda n: (0, 0)),
            pl.BlockSpec((tile, width), lambda n: (n, 0)),
        ],
        out_specs=pl.BlockSpec((rows, tile), lambda n: (0, n)),
        out_shape=jax.ShapeDtypeStruct((rows, features), BF16),
        compiler_params=pltpu.CompilerParams(vmem_limit_bytes=58 * MIB),
        cost_estimate=pl.CostEstimate(
            flops=2 * rows * width * features, bytes_accessed=2 * width * features, transcendentals=0
        ),
        name="project",
    )(gated, weight)


def on_device(queries, keys_in, values_in, filters, skip_gain, out_weight):
    count = lax.axis_size("ctx")
    rows, width = queries.shape[1:]
    cols = width // count
    table = [jnp.asarray(t) for t in tables()]
    weight = lax.all_gather(out_weight.T, ("dp", "ctx"), axis=0, tiled=True)
    product = product_blocks(keys_in[0], values_in[0], count)
    piece = lax.all_to_all(product, "ctx", split_axis=0, concat_axis=0, tiled=True)
    spec = filter_spectrum(filters, table[0], table[1])
    skip = lax.dynamic_slice_in_dim(skip_gain, lax.axis_index("ctx") * cols, cols).reshape(1, cols)
    mixed = convolve(piece.reshape(count * rows, cols), spec, skip, table)
    returned = lax.all_to_all(mixed.reshape(count, rows, cols), "ctx", split_axis=0, concat_axis=0, tiled=True)
    return project(gate(queries[0], returned), weight)[None]


def solution(mesh):
    in_specs = (
        P("dp", "ctx", None),
        P("dp", "ctx", None),
        P("dp", "ctx", None),
        P("ctx", None),
        P(),
        P(None, ("dp", "ctx")),
    )
    return jax.shard_map(
        on_device, mesh=mesh, in_specs=in_specs, out_specs=P("dp", "ctx", None), check_vma=False
    )
```

```python
import math

import jax
import jax.numpy as jnp
import ml_dtypes
import numpy as np
from jax import lax
from jax.experimental import pallas as pl
from jax.experimental.pallas import tpu as pltpu
from jax.sharding import Mesh
from jax.sharding import PartitionSpec as P

F32 = jnp.float32
BF16 = jnp.bfloat16
MIB = 1024 * 1024

OUTER = 32
INNER = 128
CHUNKS = 4


def split_table(table):
    high = table.astype(ml_dtypes.bfloat16)
    low = (table - high.astype(np.float64)).astype(ml_dtypes.bfloat16)
    return high, low


def tables():
    length = OUTER * INNER
    k1 = np.arange(OUTER)[:, None, None]
    k2 = np.arange(INNER)[None, :, None]
    b = np.arange(INNER)[None, None, :]
    theta = 2.0 * math.pi * b * (k1 + 0.25 + OUTER * k2) / length
    cos, sin = np.cos(theta), np.sin(theta)
    top = np.concatenate([cos, sin], axis=2)
    bottom = np.concatenate([-sin, cos], axis=2)
    forward = np.concatenate([top, bottom], axis=1)
    backward = np.swapaxes(forward, 1, 2) / length
    return split_table(forward) + split_table(backward)


def cadd(u, v):
    return (u[0] + v[0], u[1] + v[1])


def csub(u, v):
    return (u[0] - v[0], u[1] - v[1])


def turn(u, angle):
    quarter = round(angle / (math.pi / 2), 9)
    if quarter == int(quarter):
        quarter = int(quarter) % 4
        if quarter == 0:
            return u
        if quarter == 1:
            return (-u[1], u[0])
        if quarter == 2:
            return (-u[0], -u[1])
        return (u[1], -u[0])
    c, s = math.cos(angle), math.sin(angle)
    return (u[0] * c - u[1] * s, u[0] * s + u[1] * c)


def four(u, sign):
    p, q = cadd(u[0], u[2]), csub(u[0], u[2])
    r, t = cadd(u[1], u[3]), csub(u[1], u[3])
    if sign < 0:
        t = (t[1], -t[0])
    else:
        t = (-t[1], t[0])
    return [cadd(p, r), cadd(q, t), csub(p, r), csub(q, t)]


def eight(u, sign):
    even = four(u[0::2], sign)
    odd = four(u[1::2], sign)
    half = math.sqrt(0.5)
    o1, o3 = odd[1], odd[3]
    if sign < 0:
        odd[1] = ((o1[0] + o1[1]) * half, (o1[1] - o1[0]) * half)
        odd[2] = (odd[2][1], -odd[2][0])
        odd[3] = ((o3[1] - o3[0]) * half, (o3[0] + o3[1]) * -half)
    else:
        odd[1] = ((o1[0] - o1[1]) * half, (o1[0] + o1[1]) * half)
        odd[2] = (-odd[2][1], odd[2][0])
        odd[3] = ((o3[0] + o3[1]) * -half, (o3[0] - o3[1]) * half)
    return [cadd(even[i], odd[i]) for i in range(4)] + [csub(even[i], odd[i]) for i in range(4)]


def outer_forward(x):
    c1, s1 = math.cos(math.pi / 8), math.sin(math.pi / 8)
    half = math.sqrt(0.5)
    rows = []
    for r in range(8):
        x0, x1, x2, x3 = x[r], x[r + 8], x[r + 16], x[r + 24]
        x2 = x2 * half
        y0, y1 = (x0 + x2, -x2), (x0 - x2, x2)
        u1, v1 = x1 * c1, x1 * s1
        u3, v3 = x3 * s1, x3 * c1
        p = (u1 + u3, -(v1 + v3))
        d = (u1 - u3, v3 - v1)
        d = (d[1], -d[0])
        rows.append([cadd(y0, p), cadd(y1, d), csub(y0, p), csub(y1, d)])
    out = [None] * OUTER
    for q in range(4):
        column = [turn(rows[r][q], -2.0 * math.pi * r * (q + 0.25) / OUTER) for r in range(8)]
        for k, value in enumerate(eight(column, -1)):
            out[q + 4 * k] = value
    return out


def outer_backward(t):
    columns = []
    for q in range(4):
        g = eight([t[q + 4 * k] for k in range(8)], 1)
        columns.append([turn(g[r], 2.0 * math.pi * r * (q + 0.25) / OUTER) for r in range(8)])
    out = [None] * OUTER
    for r in range(8):
        v = [columns[q][r] for q in range(4)]
        p, s = cadd(v[0], v[2]), csub(v[0], v[2])
        w, d = cadd(v[1], v[3]), csub(v[1], v[3])
        out[r] = p[0] + w[0]
        for j, (re, im) in (
            (1, (s[0] - d[1], s[1] + d[0])),
            (2, csub(p, w)),
            (3, (s[0] + d[1], s[1] - d[0])),
        ):
            c, n = math.cos(math.pi * j / 8), math.sin(math.pi * j / 8)
            out[r + 8 * j] = re * c - im * n
    return out


def split(value):
    high = value.astype(BF16)
    return high, (value - high.astype(F32)).astype(BF16)


def close_dot(high, low, value):
    value_high, value_low = split(value)
    return (
        jnp.dot(high, value_high, preferred_element_type=F32)
        + jnp.dot(high, value_low, preferred_element_type=F32)
        + jnp.dot(low, value_high, preferred_element_type=F32)
    )


def product_kernel(keys_ref, values_ref, out_ref):
    parts, _, cols = out_ref.shape
    for j in range(parts):
        col = pl.ds(j * cols, cols)
        out_ref[j] = (keys_ref[:, col].astype(F32) * values_ref[:, col].astype(F32)).astype(BF16)


def product_blocks(keys, values, parts):
    rows, width = keys.shape
    cols = width // parts
    tile = 64
    return pl.pallas_call(
        product_kernel,
        grid=(rows // tile,),
        in_specs=[pl.BlockSpec((tile, width), lambda j: (j, 0))] * 2,
        out_specs=pl.BlockSpec((parts, tile, cols), lambda j: (0, j, 0)),
        out_shape=jax.ShapeDtypeStruct((parts, rows, cols), BF16),
        cost_estimate=pl.CostEstimate(flops=rows * width, bytes_accessed=6 * rows * width, transcendentals=0),
        name="product",
    )(keys, values)


def spectrum_kernel(filters_ref, high_ref, low_ref, out_ref, taps, high, low, sems):
    chunks = CHUNKS
    step = OUTER // chunks

    def fetch(i):
        part = pl.ds(i * step, step)
        return (
            pltpu.make_async_copy(high_ref.at[part], high.at[part], sems.at[0, i]),
            pltpu.make_async_copy(low_ref.at[part], low.at[part], sems.at[1, i]),
        )

    for i in range(chunks):
        for copy in fetch(i):
            copy.start()
    for a in range(OUTER):
        taps[pl.ds(a * INNER, INNER), :] = filters_ref[:, pl.ds(a * INNER, INNER)].T

    def outer(i, carry):
        base = pl.multiple_of(i * 8, 8)
        x = [taps[pl.ds(a * INNER + base, 8), :] for a in range(OUTER)]
        for k, (re, im) in enumerate(outer_forward(x)):
            out_ref[k, pl.ds(base, 8), :] = re
            out_ref[k, pl.ds(INNER + base, 8), :] = im
        return carry

    lax.fori_loop(0, INNER // 8, outer, 0)
    for i in range(chunks):
        for copy in fetch(i):
            copy.wait()

        def inner(k, carry):
            out_ref[k] = close_dot(high[k], low[k], out_ref[k])
            return carry

        lax.fori_loop(i * step, (i + 1) * step, inner, 0, unroll=step)


def filter_spectrum(filters, high, low):
    channels, length = filters.shape
    lanes = 128
    size = 2 * INNER
    return pl.pallas_call(
        spectrum_kernel,
        grid=(channels // lanes,),
        in_specs=[
            pl.BlockSpec((lanes, length), lambda j: (j, 0)),
            pl.BlockSpec(memory_space=pl.ANY),
            pl.BlockSpec(memory_space=pl.ANY),
        ],
        out_specs=pl.BlockSpec((OUTER, size, lanes), lambda j: (0, 0, j)),
        out_shape=jax.ShapeDtypeStruct((OUTER, size, channels), F32),
        scratch_shapes=[
            pltpu.VMEM((length, lanes), F32),
            pltpu.VMEM((OUTER, size, size), BF16),
            pltpu.VMEM((OUTER, size, size), BF16),
            pltpu.SemaphoreType.DMA((2, CHUNKS)),
        ],
        compiler_params=pltpu.CompilerParams(vmem_limit_bytes=40 * MIB),
        cost_estimate=pl.CostEstimate(
            flops=6 * OUTER * size * size * channels, bytes_accessed=16 * OUTER * size * size, transcendentals=0
        ),
        name="spectrum",
    )(filters, high, low)


def conv_kernel(
    signal_ref, spec_ref, skip_ref, fh_ref, fl_ref, bh_ref, bl_ref, out_ref, work, spec, fh, fl, bh, bl, sems
):
    chunks = CHUNKS
    step = OUTER // chunks
    lanes = 128
    channels = out_ref.shape[1]
    pairs = ((fh_ref, fh), (fl_ref, fl), (spec_ref, spec), (bh_ref, bh), (bl_ref, bl))

    def fetch(i):
        part = pl.ds(i * step, step)
        return [
            pltpu.make_async_copy(source.at[part], target.at[part], sems.at[n, i])
            for n, (source, target) in enumerate(pairs)
        ]

    for i in range(chunks):
        for copy in fetch(i):
            copy.start()

    for c in range(0, channels, lanes):
        col = pl.ds(c, lanes)

        def outer(i, carry):
            base = pl.multiple_of(i * 16, 16)
            rows = [signal_ref[pl.ds(a * INNER + base, 16), col].astype(F32) for a in range(OUTER)]
            for h in range(0, 16, 8):
                for k, (re, im) in enumerate(outer_forward([row[h : h + 8] for row in rows])):
                    work[k, pl.ds(base + h, 8), col] = re
                    work[k, pl.ds(INNER + base + h, 8), col] = im
            return carry

        lax.fori_loop(0, INNER // 16, outer, 0)

    for i in range(chunks):
        for copy in fetch(i):
            copy.wait()

        def inner(k, carry):
            value = close_dot(fh[k], fl[k], work[k])
            re, im = value[:INNER], value[INNER:]
            sre, sim = spec[k, :INNER], spec[k, INNER:]
            mixed = jnp.concatenate([re * sre - im * sim, re * sim + im * sre], axis=0)
            work[k] = close_dot(bh[k], bl[k], mixed)
            return carry

        lax.fori_loop(i * step, (i + 1) * step, inner, 0, unroll=step)

    for c in range(0, channels, lanes):
        col = pl.ds(c, lanes)
        gain = skip_ref[:, col]

        def back(i, carry):
            base = pl.multiple_of(i * 16, 16)
            halves = []
            for h in range(0, 16, 8):
                t = [
                    (work[k, pl.ds(base + h, 8), col], work[k, pl.ds(INNER + base + h, 8), col])
                    for k in range(OUTER)
                ]
                halves.append(outer_backward(t))
            for a in range(OUTER):
                rows = pl.ds(a * INNER + base, 16)
                causal = jnp.concatenate([halves[0][a], halves[1][a]], axis=0)
                out_ref[rows, col] = (causal + gain * signal_ref[rows, col].astype(F32)).astype(BF16)
            return carry

        lax.fori_loop(0, INNER // 16, back, 0)


def convolve(signal, spec, skip, table):
    length, channels = signal.shape
    size = 2 * INNER
    anywhere = pl.BlockSpec(memory_space=pl.ANY)
    inside = pl.BlockSpec(memory_space=pltpu.VMEM)
    square = pltpu.VMEM((OUTER, size, size), BF16)
    return pl.pallas_call(
        conv_kernel,
        in_specs=[inside, anywhere, inside] + [anywhere] * 4,
        out_specs=inside,
        out_shape=jax.ShapeDtypeStruct((length, channels), BF16),
        scratch_shapes=[
            pltpu.VMEM((OUTER, size, channels), F32),
            pltpu.VMEM((OUTER, size, channels), F32),
            square,
            square,
            square,
            square,
            pltpu.SemaphoreType.DMA((5, CHUNKS)),
        ],
        compiler_params=pltpu.CompilerParams(vmem_limit_bytes=48 * MIB),
        cost_estimate=pl.CostEstimate(
            flops=12 * OUTER * size * size * channels, bytes_accessed=24 * OUTER * size * size, transcendentals=0
        ),
        name="convolve",
    )(signal, spec, skip, *table)


def gate_kernel(queries_ref, mixed_ref, out_ref):
    parts, _, width = mixed_ref.shape
    for j in range(parts):
        cols = pl.ds(j * width, width)
        out_ref[:, cols] = (queries_ref[:, cols].astype(F32) * mixed_ref[j].astype(F32)).astype(BF16)


def gate(queries, mixed):
    rows, width = queries.shape
    parts, _, cols = mixed.shape
    tile = 64
    return pl.pallas_call(
        gate_kernel,
        grid=(rows // tile,),
        in_specs=[
            pl.BlockSpec((tile, width), lambda j: (j, 0)),
            pl.BlockSpec((parts, tile, cols), lambda j: (0, j, 0)),
        ],
        out_specs=pl.BlockSpec((tile, width), lambda j: (j, 0)),
        out_shape=jax.ShapeDtypeStruct((rows, width), BF16),
        cost_estimate=pl.CostEstimate(flops=rows * width, bytes_accessed=6 * rows * width, transcendentals=0),
        name="gate",
    )(queries, mixed)


def project_kernel(core_ref, gated_ref, weight_ref, own_ref, other_ref):
    rows = own_ref.shape[0]
    result = lax.dot_general(
        gated_ref[...], weight_ref[...], (((1,), (1,)), ((), ())), preferred_element_type=F32
    ).astype(BF16)
    own_ref[...] = result[:rows]
    other_ref[...] = result[rows:]


def project(gated, weight, core):
    both, width = gated.shape
    rows = both // 2
    columns = weight.shape[0]
    tile = columns // 4
    return pl.pallas_call(
        project_kernel,
        grid_spec=pltpu.PrefetchScalarGridSpec(
            num_scalar_prefetch=1,
            grid=(4,),
            in_specs=[
                pl.BlockSpec((both, width), lambda n, core: (0, 0)),
                pl.BlockSpec((tile, width), lambda n, core: (n, 0)),
            ],
            out_specs=[
                pl.BlockSpec((rows, tile), lambda n, core: (0, 2 * n + core[0])),
                pl.BlockSpec((rows, tile), lambda n, core: (0, n)),
            ],
        ),
        out_shape=[
            jax.ShapeDtypeStruct((rows, 2 * columns), BF16),
            jax.ShapeDtypeStruct((rows, columns), BF16),
        ],
        compiler_params=pltpu.CompilerParams(vmem_limit_bytes=58 * MIB),
        cost_estimate=pl.CostEstimate(
            flops=2 * both * width * columns, bytes_accessed=2 * width * columns, transcendentals=0
        ),
        name="project",
    )(core, gated, weight)


def fill_kernel(core_ref, part_ref, whole_ref, out_ref):
    del core_ref, whole_ref
    out_ref[...] = part_ref[...]


def fill(whole, part, core):
    rows, columns = part.shape
    tile = columns // 4
    return pl.pallas_call(
        fill_kernel,
        grid_spec=pltpu.PrefetchScalarGridSpec(
            num_scalar_prefetch=1,
            grid=(4,),
            in_specs=[
                pl.BlockSpec((rows, tile), lambda n, core: (0, n)),
                pl.BlockSpec(memory_space=pl.ANY),
            ],
            out_specs=pl.BlockSpec((rows, tile), lambda n, core: (0, 2 * n + 1 - core[0])),
        ),
        out_shape=jax.ShapeDtypeStruct(whole.shape, BF16),
        input_output_aliases={2: 0},
        name="fill",
    )(core, part, whole)


def on_device(queries, keys_in, values_in, filters, skip_gain, out_weight):
    count = lax.axis_size("ctx")
    rows, width = queries.shape[1:]
    cols = width // count
    table = [jnp.asarray(t) for t in tables()]
    weight = lax.all_gather(out_weight.T, ("y", "ctx"), axis=0, tiled=True)
    product = product_blocks(keys_in[0], values_in[0], count)
    piece = lax.all_to_all(product, "ctx", split_axis=0, concat_axis=0, tiled=True)
    spec = filter_spectrum(filters, table[0], table[1])
    skip = lax.dynamic_slice_in_dim(skip_gain, lax.axis_index("ctx") * cols, cols).reshape(1, cols)
    mixed = convolve(piece.reshape(count * rows, cols), spec, skip, table)
    returned = lax.all_to_all(mixed.reshape(count, rows, cols), "ctx", split_axis=0, concat_axis=0, tiled=True)
    cores = [(0, 1), (1, 0)]
    own = gate(queries[0], returned)
    other = lax.ppermute(own, "core", cores)
    core = lax.axis_index("core").astype(jnp.int32).reshape(1)
    whole, apart = project(jnp.concatenate([own, other], axis=0), weight, core)
    return fill(whole, lax.ppermute(apart, "core", cores), core)[None]


def solution(mesh):
    chips = Mesh(mesh.devices.reshape(4, 2, 16), ("y", "core", "ctx"))
    dp = ("y", "core")
    in_specs = (
        P(dp, "ctx", None),
        P(dp, "ctx", None),
        P(dp, "ctx", None),
        P("ctx", None),
        P(),
        P(None, dp + ("ctx",)),
    )
    return jax.shard_map(
        on_device, mesh=chips, in_specs=in_specs, out_specs=P(dp, "ctx", None), check_vma=False
    )
```

```python
import math

import jax
import jax.numpy as jnp
import ml_dtypes
import numpy as np
from jax import lax
from jax.experimental import pallas as pl
from jax.experimental.pallas import tpu as pltpu
from jax.sharding import Mesh
from jax.sharding import PartitionSpec as P

F32 = jnp.float32
BF16 = jnp.bfloat16
MIB = 1024 * 1024

OUTER = 32
INNER = 128
CHUNKS = 4


def split_table(table):
    high = table.astype(ml_dtypes.bfloat16)
    low = (table - high.astype(np.float64)).astype(ml_dtypes.bfloat16)
    return high, low


def tables():
    length = OUTER * INNER
    k1 = np.arange(OUTER)[:, None, None]
    k2 = np.arange(INNER)[None, :, None]
    b = np.arange(INNER)[None, None, :]
    theta = 2.0 * math.pi * b * (k1 + 0.25 + OUTER * k2) / length
    cos, sin = np.cos(theta), np.sin(theta)
    top = np.concatenate([cos, sin], axis=2)
    bottom = np.concatenate([-sin, cos], axis=2)
    forward = np.concatenate([top, bottom], axis=1)
    backward = np.swapaxes(forward, 1, 2) / length
    return split_table(forward) + split_table(backward)


def cadd(u, v):
    return (u[0] + v[0], u[1] + v[1])


def csub(u, v):
    return (u[0] - v[0], u[1] - v[1])


def turn(u, angle):
    quarter = round(angle / (math.pi / 2), 9)
    if quarter == int(quarter):
        quarter = int(quarter) % 4
        if quarter == 0:
            return u
        if quarter == 1:
            return (-u[1], u[0])
        if quarter == 2:
            return (-u[0], -u[1])
        return (u[1], -u[0])
    c, s = math.cos(angle), math.sin(angle)
    return (u[0] * c - u[1] * s, u[0] * s + u[1] * c)


def four(u, sign):
    p, q = cadd(u[0], u[2]), csub(u[0], u[2])
    r, t = cadd(u[1], u[3]), csub(u[1], u[3])
    if sign < 0:
        t = (t[1], -t[0])
    else:
        t = (-t[1], t[0])
    return [cadd(p, r), cadd(q, t), csub(p, r), csub(q, t)]


def eight(u, sign):
    even = four(u[0::2], sign)
    odd = four(u[1::2], sign)
    half = math.sqrt(0.5)
    o1, o3 = odd[1], odd[3]
    if sign < 0:
        odd[1] = ((o1[0] + o1[1]) * half, (o1[1] - o1[0]) * half)
        odd[2] = (odd[2][1], -odd[2][0])
        odd[3] = ((o3[1] - o3[0]) * half, (o3[0] + o3[1]) * -half)
    else:
        odd[1] = ((o1[0] - o1[1]) * half, (o1[0] + o1[1]) * half)
        odd[2] = (-odd[2][1], odd[2][0])
        odd[3] = ((o3[0] + o3[1]) * -half, (o3[0] - o3[1]) * half)
    return [cadd(even[i], odd[i]) for i in range(4)] + [csub(even[i], odd[i]) for i in range(4)]


def outer_forward(x):
    c1, s1 = math.cos(math.pi / 8), math.sin(math.pi / 8)
    half = math.sqrt(0.5)
    rows = []
    for r in range(8):
        x0, x1, x2, x3 = x[r], x[r + 8], x[r + 16], x[r + 24]
        x2 = x2 * half
        y0, y1 = (x0 + x2, -x2), (x0 - x2, x2)
        u1, v1 = x1 * c1, x1 * s1
        u3, v3 = x3 * s1, x3 * c1
        p = (u1 + u3, -(v1 + v3))
        d = (u1 - u3, v3 - v1)
        d = (d[1], -d[0])
        rows.append([cadd(y0, p), cadd(y1, d), csub(y0, p), csub(y1, d)])
    out = [None] * OUTER
    for q in range(4):
        column = [turn(rows[r][q], -2.0 * math.pi * r * (q + 0.25) / OUTER) for r in range(8)]
        for k, value in enumerate(eight(column, -1)):
            out[q + 4 * k] = value
    return out


def outer_backward(t):
    columns = []
    for q in range(4):
        g = eight([t[q + 4 * k] for k in range(8)], 1)
        columns.append([turn(g[r], 2.0 * math.pi * r * (q + 0.25) / OUTER) for r in range(8)])
    out = [None] * OUTER
    for r in range(8):
        v = [columns[q][r] for q in range(4)]
        p, s = cadd(v[0], v[2]), csub(v[0], v[2])
        w, d = cadd(v[1], v[3]), csub(v[1], v[3])
        out[r] = p[0] + w[0]
        for j, (re, im) in (
            (1, (s[0] - d[1], s[1] + d[0])),
            (2, csub(p, w)),
            (3, (s[0] + d[1], s[1] - d[0])),
        ):
            c, n = math.cos(math.pi * j / 8), math.sin(math.pi * j / 8)
            out[r + 8 * j] = re * c - im * n
    return out


def split(value):
    high = value.astype(BF16)
    return high, (value - high.astype(F32)).astype(BF16)


def close_dot(high, low, value):
    value_high, value_low = split(value)
    return (
        jnp.dot(high, value_high, preferred_element_type=F32)
        + jnp.dot(high, value_low, preferred_element_type=F32)
        + jnp.dot(low, value_high, preferred_element_type=F32)
    )


def product_kernel(keys_ref, values_ref, out_ref):
    parts, _, cols = out_ref.shape
    for j in range(parts):
        col = pl.ds(j * cols, cols)
        out_ref[j] = (keys_ref[:, col].astype(F32) * values_ref[:, col].astype(F32)).astype(BF16)


def product_blocks(keys, values, parts):
    rows, width = keys.shape
    cols = width // parts
    tile = 64
    return pl.pallas_call(
        product_kernel,
        grid=(rows // tile,),
        in_specs=[pl.BlockSpec((tile, width), lambda j: (j, 0))] * 2,
        out_specs=pl.BlockSpec((parts, tile, cols), lambda j: (0, j, 0)),
        out_shape=jax.ShapeDtypeStruct((parts, rows, cols), BF16),
        cost_estimate=pl.CostEstimate(flops=rows * width, bytes_accessed=6 * rows * width, transcendentals=0),
        name="product",
    )(keys, values)


def spectrum_kernel(filters_ref, high_ref, low_ref, out_ref, taps, high, low, sems):
    chunks = CHUNKS
    step = OUTER // chunks

    def fetch(i):
        part = pl.ds(i * step, step)
        return (
            pltpu.make_async_copy(high_ref.at[part], high.at[part], sems.at[0, i]),
            pltpu.make_async_copy(low_ref.at[part], low.at[part], sems.at[1, i]),
        )

    for i in range(chunks):
        for copy in fetch(i):
            copy.start()
    for a in range(OUTER):
        taps[pl.ds(a * INNER, INNER), :] = filters_ref[:, pl.ds(a * INNER, INNER)].T

    def outer(i, carry):
        base = pl.multiple_of(i * 8, 8)
        x = [taps[pl.ds(a * INNER + base, 8), :] for a in range(OUTER)]
        for k, (re, im) in enumerate(outer_forward(x)):
            out_ref[k, pl.ds(base, 8), :] = re
            out_ref[k, pl.ds(INNER + base, 8), :] = im
        return carry

    lax.fori_loop(0, INNER // 8, outer, 0)
    for i in range(chunks):
        for copy in fetch(i):
            copy.wait()

        def inner(k, carry):
            out_ref[k] = close_dot(high[k], low[k], out_ref[k])
            return carry

        lax.fori_loop(i * step, (i + 1) * step, inner, 0, unroll=step)


def filter_spectrum(filters, high, low):
    channels, length = filters.shape
    lanes = 128
    size = 2 * INNER
    return pl.pallas_call(
        spectrum_kernel,
        grid=(channels // lanes,),
        in_specs=[
            pl.BlockSpec((lanes, length), lambda j: (j, 0)),
            pl.BlockSpec(memory_space=pl.ANY),
            pl.BlockSpec(memory_space=pl.ANY),
        ],
        out_specs=pl.BlockSpec((OUTER, size, lanes), lambda j: (0, 0, j)),
        out_shape=jax.ShapeDtypeStruct((OUTER, size, channels), F32),
        scratch_shapes=[
            pltpu.VMEM((length, lanes), F32),
            pltpu.VMEM((OUTER, size, size), BF16),
            pltpu.VMEM((OUTER, size, size), BF16),
            pltpu.SemaphoreType.DMA((2, CHUNKS)),
        ],
        compiler_params=pltpu.CompilerParams(vmem_limit_bytes=40 * MIB),
        cost_estimate=pl.CostEstimate(
            flops=6 * OUTER * size * size * channels, bytes_accessed=16 * OUTER * size * size, transcendentals=0
        ),
        name="spectrum",
    )(filters, high, low)


def conv_kernel(
    signal_ref, spec_ref, skip_ref, fh_ref, fl_ref, bh_ref, bl_ref, out_ref, work, spec, fh, fl, bh, bl, sems
):
    chunks = CHUNKS
    step = OUTER // chunks
    lanes = 128
    channels = out_ref.shape[1]
    pairs = ((fh_ref, fh), (fl_ref, fl), (spec_ref, spec), (bh_ref, bh), (bl_ref, bl))

    def fetch(i):
        part = pl.ds(i * step, step)
        return [
            pltpu.make_async_copy(source.at[part], target.at[part], sems.at[n, i])
            for n, (source, target) in enumerate(pairs)
        ]

    for i in range(chunks):
        for copy in fetch(i):
            copy.start()

    for c in range(0, channels, lanes):
        col = pl.ds(c, lanes)

        def outer(i, carry):
            base = pl.multiple_of(i * 16, 16)
            rows = [signal_ref[pl.ds(a * INNER + base, 16), col].astype(F32) for a in range(OUTER)]
            for h in range(0, 16, 8):
                for k, (re, im) in enumerate(outer_forward([row[h : h + 8] for row in rows])):
                    work[k, pl.ds(base + h, 8), col] = re
                    work[k, pl.ds(INNER + base + h, 8), col] = im
            return carry

        lax.fori_loop(0, INNER // 16, outer, 0)

    for i in range(chunks):
        for copy in fetch(i):
            copy.wait()

        def inner(k, carry):
            value = close_dot(fh[k], fl[k], work[k])
            re, im = value[:INNER], value[INNER:]
            sre, sim = spec[k, :INNER], spec[k, INNER:]
            mixed = jnp.concatenate([re * sre - im * sim, re * sim + im * sre], axis=0)
            work[k] = close_dot(bh[k], bl[k], mixed)
            return carry

        lax.fori_loop(i * step, (i + 1) * step, inner, 0, unroll=step)

    for c in range(0, channels, lanes):
        col = pl.ds(c, lanes)
        gain = skip_ref[:, col]

        def back(i, carry):
            base = pl.multiple_of(i * 16, 16)
            halves = []
            for h in range(0, 16, 8):
                t = [
                    (work[k, pl.ds(base + h, 8), col], work[k, pl.ds(INNER + base + h, 8), col])
                    for k in range(OUTER)
                ]
                halves.append(outer_backward(t))
            for a in range(OUTER):
                rows = pl.ds(a * INNER + base, 16)
                causal = jnp.concatenate([halves[0][a], halves[1][a]], axis=0)
                out_ref[rows, col] = (causal + gain * signal_ref[rows, col].astype(F32)).astype(BF16)
            return carry

        lax.fori_loop(0, INNER // 16, back, 0)


def convolve(signal, spec, skip, table):
    length, channels = signal.shape
    size = 2 * INNER
    anywhere = pl.BlockSpec(memory_space=pl.ANY)
    inside = pl.BlockSpec(memory_space=pltpu.VMEM)
    square = pltpu.VMEM((OUTER, size, size), BF16)
    return pl.pallas_call(
        conv_kernel,
        in_specs=[inside, anywhere, inside] + [anywhere] * 4,
        out_specs=inside,
        out_shape=jax.ShapeDtypeStruct((length, channels), BF16),
        scratch_shapes=[
            pltpu.VMEM((OUTER, size, channels), F32),
            pltpu.VMEM((OUTER, size, channels), F32),
            square,
            square,
            square,
            square,
            pltpu.SemaphoreType.DMA((5, CHUNKS)),
        ],
        compiler_params=pltpu.CompilerParams(vmem_limit_bytes=48 * MIB),
        cost_estimate=pl.CostEstimate(
            flops=12 * OUTER * size * size * channels, bytes_accessed=24 * OUTER * size * size, transcendentals=0
        ),
        name="convolve",
    )(signal, spec, skip, *table)


def gate_kernel(queries_ref, mixed_ref, out_ref):
    parts, _, width = mixed_ref.shape
    for j in range(parts):
        cols = pl.ds(j * width, width)
        out_ref[:, cols] = (queries_ref[:, cols].astype(F32) * mixed_ref[j].astype(F32)).astype(BF16)


def gate(queries, mixed):
    rows, width = queries.shape
    parts, _, cols = mixed.shape
    tile = 64
    return pl.pallas_call(
        gate_kernel,
        grid=(rows // tile,),
        in_specs=[
            pl.BlockSpec((tile, width), lambda j: (j, 0)),
            pl.BlockSpec((parts, tile, cols), lambda j: (0, j, 0)),
        ],
        out_specs=pl.BlockSpec((tile, width), lambda j: (j, 0)),
        out_shape=jax.ShapeDtypeStruct((rows, width), BF16),
        cost_estimate=pl.CostEstimate(flops=rows * width, bytes_accessed=6 * rows * width, transcendentals=0),
        name="gate",
    )(queries, mixed)


def project_kernel(core_ref, gated_ref, weight_ref, own_ref, other_ref):
    rows = own_ref.shape[0]
    result = lax.dot_general(
        gated_ref[...], weight_ref[...], (((1,), (1,)), ((), ())), preferred_element_type=F32
    ).astype(BF16)
    own_ref[...] = result[:rows]
    other_ref[...] = result[rows:]


def project(gated, weight, core):
    both, width = gated.shape
    rows = both // 2
    columns = weight.shape[0]
    tile = columns // 4
    return pl.pallas_call(
        project_kernel,
        grid_spec=pltpu.PrefetchScalarGridSpec(
            num_scalar_prefetch=1,
            grid=(4,),
            in_specs=[
                pl.BlockSpec((both, width), lambda n, core: (0, 0)),
                pl.BlockSpec((tile, width), lambda n, core: (n, 0)),
            ],
            out_specs=[
                pl.BlockSpec((rows, tile), lambda n, core: (0, 2 * n + core[0])),
                pl.BlockSpec((rows, tile), lambda n, core: (0, n)),
            ],
        ),
        out_shape=[
            jax.ShapeDtypeStruct((rows, 2 * columns), BF16),
            jax.ShapeDtypeStruct((rows, columns), BF16),
        ],
        compiler_params=pltpu.CompilerParams(vmem_limit_bytes=58 * MIB),
        cost_estimate=pl.CostEstimate(
            flops=2 * both * width * columns, bytes_accessed=2 * width * columns, transcendentals=0
        ),
        name="project",
    )(core, gated, weight)


def fill_kernel(core_ref, part_ref, whole_ref, out_ref, sems):
    del whole_ref
    tile = part_ref.shape[1] // 4
    copies = []
    for n in range(4):
        start = pl.multiple_of((2 * n + 1 - core_ref[0]) * tile, tile)
        copies.append(
            pltpu.make_async_copy(part_ref.at[:, pl.ds(n * tile, tile)], out_ref.at[:, pl.ds(start, tile)], sems.at[n])
        )
    for copy in copies:
        copy.start()
    for copy in copies:
        copy.wait()


def fill(whole, part, core):
    anywhere = pl.BlockSpec(memory_space=pl.ANY)
    return pl.pallas_call(
        fill_kernel,
        in_specs=[pl.BlockSpec(memory_space=pltpu.SMEM), anywhere, anywhere],
        out_specs=anywhere,
        out_shape=jax.ShapeDtypeStruct(whole.shape, BF16),
        scratch_shapes=[pltpu.SemaphoreType.DMA((4,))],
        input_output_aliases={2: 0},
        compiler_params=pltpu.CompilerParams(vmem_limit_bytes=58 * MIB),
        name="fill",
    )(core, part, whole)


def on_device(queries, keys_in, values_in, filters, skip_gain, out_weight):
    count = lax.axis_size("ctx")
    rows, width = queries.shape[1:]
    cols = width // count
    table = [jnp.asarray(t) for t in tables()]
    weight = lax.all_gather(out_weight.T, ("y", "ctx"), axis=0, tiled=True)
    product = product_blocks(keys_in[0], values_in[0], count)
    piece = lax.all_to_all(product, "ctx", split_axis=0, concat_axis=0, tiled=True)
    spec = filter_spectrum(filters, table[0], table[1])
    skip = lax.dynamic_slice_in_dim(skip_gain, lax.axis_index("ctx") * cols, cols).reshape(1, cols)
    mixed = convolve(piece.reshape(count * rows, cols), spec, skip, table)
    returned = lax.all_to_all(mixed.reshape(count, rows, cols), "ctx", split_axis=0, concat_axis=0, tiled=True)
    cores = [(0, 1), (1, 0)]
    own = gate(queries[0], returned)
    other = lax.ppermute(own, "core", cores)
    core = lax.axis_index("core").astype(jnp.int32).reshape(1)
    whole, apart = project(jnp.concatenate([own, other], axis=0), weight, core)
    return fill(whole, lax.ppermute(apart, "core", cores), core)[None]


def solution(mesh):
    chips = Mesh(mesh.devices.reshape(4, 2, 16), ("y", "core", "ctx"))
    dp = ("y", "core")
    in_specs = (
        P(dp, "ctx", None),
        P(dp, "ctx", None),
        P(dp, "ctx", None),
        P("ctx", None),
        P(),
        P(None, dp + ("ctx",)),
    )
    return jax.shard_map(
        on_device, mesh=chips, in_specs=in_specs, out_specs=P(dp, "ctx", None), check_vma=False
    )
```
